256 devices in a mesh: section: 16 (over y, x), dp: 16 (over z, core).
Axes of the slice: x: 4, y: 4, z: 8, core: 2. Of those that a mesh axis runs over, the one named last changes fastest.
Arguments:
- inputs: bfloat16 [64, 32, 2304], P('dp'), may hold values from -6 to 6
- value_weight: bfloat16 [16, 2304, 2048], P('section'), may hold values from -0.25 to 0.25
- output_weight: bfloat16 [16, 2304, 2048], P('section', 'dp'), may hold values from -0.125 to 0.125
- cotangent: bfloat16 [64, 32, 2304], P('dp'), may hold values from -40 to 40
- lengths: int32 [64], P('dp'), may hold values from 8 to 32
Outputs:
- clipped_gradient: bfloat16 [16, 2304, 2048], P('section', 'dp')
The draws below stay inside these ranges and needn't reach their ends.
All inputs are finite; a program needn't handle non-finite values.
Results may differ from the reference program's by a relative error of at most 0.03.
Values may be sent and summed in bfloat16 or wider, within the bound.
A program may use at most 128 MiB of HBM per device.

```python
import math
import jax
import jax.numpy as jnp
from jax import lax

D = 2304
SEQ = 32
EX_DEV = 4
FV = 2048
LAYERS = 16
EXAMPLES = 64
N_DP = 16


def draw_inputs(key, part):
    key = jax.random.fold_in(key, 5)
    key_list = jax.random.split(key, 2)
    own = jax.random.truncated_normal(key_list[0], -4.0, 4.0, (EXAMPLES, SEQ, D), jnp.float32)
    shared = jax.random.truncated_normal(key_list[1], -4.0, 4.0, (EXAMPLES, 1, D), jnp.float32)
    base = 0.6 * own + 0.8 * shared
    return base.astype(jnp.bfloat16)


def draw_value_weight(key, part):
    key = jax.random.fold_in(key, 11)
    depth = jnp.arange(LAYERS, dtype=jnp.float32)[:, None, None] / (LAYERS - 1)
    base = jax.random.truncated_normal(key, -4.0, 4.0, (LAYERS, D, FV), jnp.float32)
    growth = 1.0 + 2.0 * depth
    return (base * growth / math.sqrt(D)).astype(jnp.bfloat16)


def draw_cotangent(key, part):
    key = jax.random.fold_in(key, 23)
    key_list = jax.random.split(key, 5)
    row_scale = jnp.exp(jax.random.uniform(key_list[0], (EXAMPLES, SEQ, 1), jnp.float32, 0.0, math.log(10.0)))
    col_scale = jnp.exp(jax.random.uniform(key_list[1], (1, 1, D), jnp.float32, 0.0, math.log(10.0)))
    own = jax.random.truncated_normal(key_list[2], -4.0, 4.0, (EXAMPLES, SEQ, D), jnp.float32)
    shared = jax.random.truncated_normal(key_list[4], -4.0, 4.0, (EXAMPLES, 1, D), jnp.float32)
    base = 0.55 * own + 0.45 * shared
    return (base * row_scale * col_scale / 10.0).astype(jnp.bfloat16)


def place_ends(result, key, low, largest):
    dims = result.shape
    spot = [jax.random.randint(jax.random.fold_in(key, axis), (), 0, dims[axis]) for axis in range(len(dims))]
    result = result.at[tuple(spot)].set(low)
    longest = dims.index(max(dims))
    spot[longest] = (spot[longest] + 1) % dims[longest]
    return result.at[tuple(spot)].set(largest)


def levels(stream_key, shape, cuts, smallest, high):
    loudness, own = 1.0, jax.random.fold_in(stream_key, 6)
    for dim, shards_of in cuts:
        steps = jnp.exp(jax.random.uniform(jax.random.fold_in(own, dim), (shards_of,), jnp.float32, smallest / len(cuts), high / len(cuts)))
        loudness = loudness * jnp.repeat(steps, shape[dim] // shards_of).reshape([-1 if axis == dim else 1 for axis in range(len(shape))])
    return loudness


def normal_values(own_key, dims, spread, reach, cuts=(), kind=jnp.bfloat16):
    array = jax.random.normal(own_key, dims, jnp.float32) * spread
    if len(cuts) > 0:
        array = levels(own_key, dims, cuts, -0.22, 0.18) * array
    return jnp.clip(array, min=-reach, max=reach).astype(kind)


def setup_inputs(seed: int = 0) -> dict:
    key_of = jax.random.split(jax.random.key(seed), 6)
    return {
        "inputs": draw_inputs(jax.random.fold_in(key_of[5], 71), 0),
        "value_weight": draw_value_weight(jax.random.fold_in(key_of[5], 71), 0),
        "output_weight": normal_values(key_of[2], (LAYERS, D, FV), FV ** -0.5, 0.125, ((0, 16), (1, 16))),
        "cotangent": draw_cotangent(jax.random.fold_in(key_of[5], 71), 0),
        "lengths": place_ends(jax.random.randint(key_of[4], (EXAMPLES,), SEQ // 4, SEQ + 1), jax.random.fold_in(key_of[4], 1), SEQ // 4, SEQ).astype(jnp.int32),
    }


EPS = 1e-06
GAMMA = 0.01

def norm_parts(hidden):
    hidden_f32 = hidden.astype(jnp.float32)
    inv_rms = lax.rsqrt(lax.optimization_barrier(jnp.mean(hidden_f32 * hidden_f32, axis=-1, keepdims=True)) + EPS)
    return (hidden_f32, inv_rms, hidden_f32 * inv_rms)

def reference(inputs, value_weight, output_weight, cotangent, lengths):
    row_total = EXAMPLES * SEQ
    hidden = inputs.reshape(row_total, D)
    kept_hidden = []
    kept_values = []
    for layer in range(LAYERS):
        hidden_f32, inv_rms, normed = norm_parts(hidden)
        values = jnp.dot(normed.astype(jnp.bfloat16), value_weight[layer], preferred_element_type=jnp.float32).astype(jnp.bfloat16)
        mixed = jnp.dot(values, output_weight[layer].T, preferred_element_type=jnp.float32)
        kept_hidden.append(hidden)
        kept_values.append(values)
        hidden = (hidden_f32 + mixed).astype(jnp.bfloat16)
    is_live = jnp.arange(SEQ, dtype=jnp.int32)[None, :] < lengths[:, None]
    grad = jnp.where(is_live[:, :, None], cotangent, jnp.zeros((), jnp.bfloat16)).reshape(row_total, D)
    kept_grads = [None] * LAYERS
    norm_terms = []
    for layer in reversed(range(LAYERS)):
        kept_grads[layer] = grad
        values = kept_values[layer]
        val_three = values.astype(jnp.float32).reshape(EXAMPLES, SEQ, FV)
        grad_three = grad.astype(jnp.float32).reshape(EXAMPLES, SEQ, D)
        gram_values = jnp.einsum('etf,esf->ets', val_three, val_three)
        gram_grads = jnp.einsum('etc,esc->ets', grad_three, grad_three)
        norm_terms.append(lax.optimization_barrier(jnp.sum(gram_values * gram_grads, axis=(1, 2))))
        if layer > 0:
            hidden_f32, inv_rms, normed = norm_parts(kept_hidden[layer])
            grad_values = jnp.dot(grad, output_weight[layer], preferred_element_type=jnp.float32).astype(jnp.bfloat16)
            grad_normed = jnp.dot(grad_values, value_weight[layer].T, preferred_element_type=jnp.float32)
            inner_mean = lax.optimization_barrier(jnp.mean(grad_normed * normed, axis=-1, keepdims=True))
            grad = (grad.astype(jnp.float32) + inv_rms * (grad_normed - normed * inner_mean)).astype(jnp.bfloat16)
    totals = jnp.zeros((EXAMPLES,), jnp.float32)
    for norm_term in norm_terms:
        totals = totals + norm_term
    clip_scale = math.sqrt(FV * D / EXAMPLES)
    factors = clip_scale / (jnp.sqrt(totals) + GAMMA)
    row_factors = jnp.repeat(factors, SEQ)[:, None]
    results = []
    for layer in range(LAYERS):
        weighted = (kept_grads[layer].astype(jnp.float32) * row_factors).astype(jnp.bfloat16)
        weighted_groups = weighted.reshape(N_DP, EX_DEV * SEQ, D)
        value_groups = kept_values[layer].reshape(N_DP, EX_DEV * SEQ, FV)

        def add_group(running, pair):
            weight_part, value_part = pair
            grad_term = jnp.dot(weight_part.T, value_part, preferred_element_type=jnp.float32)
            grad_term = lax.optimization_barrier(grad_term.astype(jnp.bfloat16)).astype(jnp.float32)
            return (running + grad_term, None)
        summed, _ = lax.scan(add_group, jnp.zeros((D, FV), jnp.float32), (weighted_groups, value_groups))
        results.append(summed.astype(jnp.bfloat16))
    return jnp.stack(results)
```

```python
import functools
import math

import jax
import jax.numpy as jnp
from jax import lax
from jax.experimental import pallas as pl
from jax.experimental.pallas import tpu as pltpu
from jax.sharding import PartitionSpec as P

EPS = 1e-06
GAMMA = 0.01
MESH = pl.DeviceIdType.MESH
F32 = jnp.float32
BF16 = jnp.bfloat16


def dot_nn(a, b):
    return lax.dot_general(a, b, (((1,), (0,)), ((), ())), preferred_element_type=F32)


def dot_nt(a, b):
    return lax.dot_general(a, b, (((1,), (1,)), ((), ())), preferred_element_type=F32)


def dot_tn(a, b):
    return lax.dot_general(a, b, (((0,), (0,)), ((), ())), preferred_element_type=F32)


def pick(cond, fn):
    def run():
        fn()

    pl.when(cond)(run)


def relay_kernel(
    cfg, inp_ref, value_ref, slice_ref, cot_ref, len_ref, hk_ref, gk_ref,
    vbuf, wbuf, pbuf, tbuf, hbuf, obuf, gbuf, qbuf, ubuf,
    load_sem, sib_sem, ring_send, ring_recv, h_send, h_recv, g_send, g_recv,
    keep_send, keep_recv,
):
    secs, chips, per, width, cw, nch, tsec = cfg
    half_ring = chips // 2
    rows_sl = slice_ref.shape[0]
    count = 2 * per
    cn = width // nch
    sec = lax.axis_index("section")
    dp = lax.axis_index("dp")
    chip = lax.div(dp, 2)
    core = lax.rem(dp, 2)
    sib = (sec, dp + 1 - 2 * core)
    up = (sec, lax.rem(chip + 1, chips) * 2 + core)
    down = (sec, lax.rem(chip + chips - 1, chips) * 2 + core)
    nxt = (lax.rem(sec + 1, secs), dp)
    prv = (lax.rem(sec + secs - 1, secs), dp)
    first, last = sec == 0, sec == secs - 1

    barrier = pltpu.get_barrier_semaphore()
    for dev in (sib, up, down, nxt, prv):
        pl.semaphore_signal(barrier, inc=1, device_id=dev, device_id_type=MESH)
    pl.semaphore_wait(barrier, 5)

    def remote(src, dst, send, recv, dev):
        return pltpu.make_async_remote_copy(
            src_ref=src, dst_ref=dst, send_sem=send, recv_sem=recv, device_id=dev, device_id_type=MESH
        )

    def slice_rows(index):
        return wbuf.at[pl.ds(pl.multiple_of(index * rows_sl, 16), rows_sl), :]

    def mask_rows(slot, position):
        seq = gbuf.shape[1]
        live = lax.broadcasted_iota(jnp.int32, (seq, 1), 0) < len_ref[position]
        gbuf[slot] = jnp.where(live, gbuf[slot].astype(F32), 0.0).astype(BF16)

    def keep(src, dst_ref, kind, mb):
        def far():
            remote(src, dst_ref.at[mb], keep_send.at[kind, mb], keep_recv.at[kind, mb], sib).start()

        def near():
            pltpu.make_async_copy(src, dst_ref.at[mb - per], keep_send.at[kind, mb]).start()

        pick(mb < per, far)
        pick(mb >= per, near)

    def helper_core():
        to_sib = remote(slice_ref, slice_rows(2 * chip), sib_sem.at[0], sib_sem.at[1], sib)
        to_sib.start()

        def send_inputs():
            for i in range(per):
                remote(inp_ref.at[i], hbuf.at[i], h_send.at[i], h_recv.at[i], sib).start()
            for i in range(per):
                remote(inp_ref.at[i], hbuf.at[i], h_send.at[i], h_recv.at[i], sib).wait_send()

        def send_cot():
            for i in range(per):
                pltpu.make_async_copy(cot_ref.at[i], gbuf.at[i], load_sem.at[i]).start()
            for i in range(per):
                pltpu.make_async_copy(cot_ref.at[i], gbuf.at[i], load_sem.at[i]).wait()
                mask_rows(i, i)
                remote(gbuf.at[i], gbuf.at[i], g_send.at[i], g_recv.at[i], sib).start()
            for i in range(per):
                remote(gbuf.at[i], gbuf.at[i], g_send.at[i], g_recv.at[i], sib).wait_send()

        pick(first, send_inputs)
        pick(last, send_cot)
        to_sib.wait_send()
        for i in range(per):
            remote(hbuf.at[i], hk_ref.at[i], keep_send.at[0, i], keep_recv.at[0, i], sib).wait_recv()
            remote(gbuf.at[i], gk_ref.at[i], keep_send.at[1, i], keep_recv.at[1, i], sib).wait_recv()

    def relay_core():
        load_v = pltpu.make_async_copy(value_ref, vbuf, load_sem.at[0])
        load_w = pltpu.make_async_copy(slice_ref, slice_rows(2 * chip + 1), load_sem.at[1])
        load_in = pltpu.make_async_copy(inp_ref, hbuf.at[pl.ds(per, per)], load_sem.at[2])
        load_cot = pltpu.make_async_copy(cot_ref, gbuf.at[pl.ds(per, per)], load_sem.at[3])

        def ring(way, dist, half, src=None):
            step = dist - 1
            origin = lax.rem(chip + chips - step, chips) if way == 0 else lax.rem(chip + step, chips)
            block = slice_rows(2 * origin + half)
            dev = up if way == 0 else down
            return remote(
                block if src is None else src, block,
                ring_send.at[way, step, half], ring_recv.at[way, step, half], dev,
            )

        def arrived(way, dist, half):
            origin = lax.rem(chip + chips - dist, chips) if way == 0 else lax.rem(chip + dist, chips)
            block = slice_rows(2 * origin + half)
            remote(
                block, block, ring_send.at[way, dist - 1, half], ring_recv.at[way, dist - 1, half], up
            ).wait_recv()

        for way in range(2):
            ring(way, 1, 1, slice_ref).start()
        load_w.start()
        load_v.start()
        pick(first, load_in.start)
        pick(last, load_cot.start)
        remote(slice_ref, slice_rows(2 * chip), sib_sem.at[0], sib_sem.at[1], sib).wait_recv()
        for way in range(2):
            ring(way, 1, 0).start()
        pick(first, load_in.wait)

        def ready_cot():
            load_cot.wait()
            for i in range(per):
                mask_rows(per + i, i)

        pick(last, ready_cot)
        load_w.wait()
        load_v.wait()

        def slice_event(index):
            gap = lax.rem(lax.div(index, 2) + chips - chip, chips)
            dist = jnp.minimum(gap, chips - gap)
            near = 2 * dist - lax.rem(index, 2)
            return jnp.where(dist == 0, 0, jnp.where(dist == half_ring, 2 * half_ring - 1, near))

        def chunk_event(j):
            lo, hi = lax.div(cw * j, rows_sl), lax.div(cw * j + cw - 1, rows_sl)
            event = slice_event(lo)
            for extra in range(1, cw // rows_sl + 2):
                event = jnp.maximum(event, slice_event(jnp.minimum(lo + extra, hi)))
            return event

        def make_p(event):
            def chunk(j, _):
                def run():
                    off = pl.multiple_of(j * cw, cw)
                    for m in range(nch):
                        block = dot_nt(vbuf[m * cn:(m + 1) * cn, :], wbuf[pl.ds(off, cw), :])
                        pbuf[m * cn:(m + 1) * cn, pl.ds(off, cw)] = block.astype(BF16)

                pick(chunk_event(j) == event, run)
                return 0

            lax.fori_loop(0, width // cw, chunk, 0)

        def ring_event(e, _):
            dist, half = lax.div(e + 1, 2), lax.rem(e, 2)

            def turn():
                arrived(0, dist, half)
                pick(jnp.logical_or(dist + 1 < half_ring, half == 0), ring(0, dist + 1, half).start)
                arrived(1, dist, half)
                pick(jnp.logical_or(dist + 1 < half_ring, half == 1), ring(1, dist + 1, half).start)

            def final():
                arrived(0, half_ring, 0)
                arrived(1, half_ring, 1)

            pick(jnp.logical_and(e > 0, e < 2 * half_ring - 1), turn)
            pick(e == 2 * half_ring - 1, final)
            make_p(e)
            return 0

        lax.fori_loop(0, 2 * half_ring, ring_event, 0)

        def make_t():
            def chunk(j, _):
                off = pl.multiple_of(j * cw, cw)
                for m in range(nch):
                    block = dot_nt(wbuf[pl.ds(off, cw), :], vbuf[m * cn:(m + 1) * cn, :])
                    tbuf[pl.ds(off, cw), m * cn:(m + 1) * cn] = block.astype(BF16)
                return 0

            lax.fori_loop(0, width // cw, chunk, 0)

        pick(sec >= tsec, make_t)

        def whole(buf, mb, send, recv, dev):
            return remote(buf.at[mb], buf.at[mb], send.at[mb], recv.at[mb], dev)

        def inv_rms(h32):
            return lax.rsqrt(jnp.mean(h32 * h32, axis=-1, keepdims=True) + EPS)

        def forward(mb, _):
            pick(jnp.logical_or(sec > 0, mb < per), whole(hbuf, mb, h_send, h_recv, sib).wait_recv)
            keep(hbuf.at[mb], hk_ref, 0, mb)
            h = hbuf[mb]
            h32 = h.astype(F32)
            r = inv_rms(h32)
            for c in range(nch):
                cols = pl.ds(c * cn, cn)
                u = dot_nn(h, pbuf[:, c * cn:(c + 1) * cn])
                ubuf[mb, :, c * cn:(c + 1) * cn] = u
                obuf[mb, :, c * cn:(c + 1) * cn] = (h32[:, c * cn:(c + 1) * cn] + r * u).astype(BF16)
                remote(
                    obuf.at[mb, :, cols], hbuf.at[mb, :, cols], h_send.at[mb], h_recv.at[mb], nxt
                ).start()
            return 0

        pick(sec < secs - 1, lambda: lax.fori_loop(0, count, forward, 0))
        pick(jnp.logical_and(sec > 0, sec < tsec), make_t)

        def send_grad(mb, c):
            cols = pl.ds(c * cn, cn)
            remote(
                qbuf.at[mb, :, cols], gbuf.at[mb, :, cols], g_send.at[mb], g_recv.at[mb], prv
            ).start()

        def backward(mb, _):
            whole(gbuf, mb, g_send, g_recv, sib).wait_recv()
            keep(gbuf.at[mb], gk_ref, 1, mb)
            g = gbuf[mb]
            g32, h32 = g.astype(F32), hbuf[mb].astype(F32)
            r = inv_rms(h32)
            coef = jnp.sum(g32 * ubuf[mb], axis=-1, keepdims=True) * (r * r * r) * (1.0 / width)
            for c in range(nch):
                lo, hi = c * cn, (c + 1) * cn
                p = dot_nn(g, tbuf[:, lo:hi])
                qbuf[mb, :, lo:hi] = (g32[:, lo:hi] + r * p - coef * h32[:, lo:hi]).astype(BF16)
                send_grad(mb, c)
            return 0

        def backward_last(mb, _):
            pick(mb < per, whole(gbuf, mb, g_send, g_recv, sib).wait_recv)
            keep(gbuf.at[mb], gk_ref, 1, mb)
            whole(hbuf, mb, h_send, h_recv, sib).wait_recv()
            keep(hbuf.at[mb], hk_ref, 0, mb)
            g = gbuf[mb]
            g32, h32 = g.astype(F32), hbuf[mb].astype(F32)
            r = inv_rms(h32)
            dots = jnp.zeros_like(r)
            for c in range(nch):
                lo, hi = c * cn, (c + 1) * cn
                p = dot_nn(g, tbuf[:, lo:hi])
                ubuf[mb, :, lo:hi] = p
                dots = dots + jnp.sum(p * h32[:, lo:hi], axis=-1, keepdims=True)
            coef = dots * (r * r * r) * (1.0 / width)
            for c in range(nch):
                lo, hi = c * cn, (c + 1) * cn
                p = ubuf[mb, :, lo:hi]
                qbuf[mb, :, lo:hi] = (g32[:, lo:hi] + r * p - coef * h32[:, lo:hi]).astype(BF16)
                send_grad(mb, c)
            return 0

        def backward_first(mb, _):
            whole(gbuf, mb, g_send, g_recv, sib).wait_recv()
            keep(gbuf.at[mb], gk_ref, 1, mb)
            return 0

        pick(last, lambda: lax.fori_loop(0, count, backward_last, 0))
        pick(
            jnp.logical_and(sec > 0, sec < secs - 1),
            lambda: lax.fori_loop(0, count, backward, 0),
        )
        pick(first, lambda: lax.fori_loop(0, count, backward_first, 0))

        def drain(mb, _):
            pick(sec < secs - 1, whole(hbuf, mb, h_send, h_recv, nxt).wait_send)
            pick(sec > 0, whole(gbuf, mb, g_send, g_recv, prv).wait_send)
            for kind, buf, out in ((0, hbuf, hk_ref), (1, gbuf, gk_ref)):
                pick(mb < per, remote(buf.at[mb], out.at[0], keep_send.at[kind, mb], keep_recv.at[kind, mb], sib).wait_send)
                pick(mb >= per, pltpu.make_async_copy(buf.at[mb], out.at[0], keep_send.at[kind, mb]).wait)
            return 0

        lax.fori_loop(0, count, drain, 0)
        for way in range(2):
            for dist in range(1, half_ring + 1):
                for half in range(2):
                    if dist < half_ring or half == way:
                        ring(way, dist, half).wait_send()

    pick(core == 0, helper_core)
    pick(core == 1, relay_core)


def relay(inputs, value_weight, output_weight, cotangent, lengths, cw, nch, tsec):
    per, seq, width = inputs.shape
    features = value_weight.shape[1]
    secs, chips = lax.axis_size("section"), lax.axis_size("dp") // 2
    count = 2 * per
    any_spec = pl.BlockSpec(memory_space=pl.ANY)
    keep = jax.ShapeDtypeStruct((per, seq, width), BF16)
    dma = pltpu.SemaphoreType.DMA
    return pl.pallas_call(
        functools.partial(relay_kernel, (secs, chips, per, width, cw, nch, tsec)),
        out_shape=(keep, keep),
        in_specs=[any_spec] * 4 + [pl.BlockSpec(memory_space=pltpu.SMEM)],
        out_specs=(any_spec, any_spec),
        scratch_shapes=[
            pltpu.VMEM((width, features), BF16),
            pltpu.VMEM((width, features), BF16),
            pltpu.VMEM((width, width), BF16),
            pltpu.VMEM((width, width), BF16),
            pltpu.VMEM((count, seq, width), BF16),
            pltpu.VMEM((count, seq, width), BF16),
            pltpu.VMEM((count, seq, width), BF16),
            pltpu.VMEM((count, seq, width), BF16),
            pltpu.VMEM((count, seq, width), F32),
            dma((per + 4,)),
            dma((2,)),
            dma((2, chips // 2, 2)),
            dma((2, chips // 2, 2)),
            dma((count,)),
            dma((count,)),
            dma((count,)),
            dma((count,)),
            dma((2, count)),
            dma((2, count)),
        ],
        compiler_params=pltpu.CompilerParams(
            collective_id=0, has_side_effects=True, vmem_limit_bytes=60 << 20
        ),
    )(inputs, value_weight, output_weight, cotangent, lengths)


def per_device(inputs, value_weight, output_weight, cotangent, lengths, cw=256, nch=3, tsec=10):
    per, seq, width = inputs.shape
    w_value = value_weight[0]
    features = w_value.shape[1]
    clip_scale = math.sqrt(features * width * 1.0 / (per * lax.axis_size("dp")))
    hidden, grads = relay(inputs, w_value, output_weight[0], cotangent, lengths, cw, nch, tsec)
    h32 = hidden.astype(F32)
    normed = (h32 * lax.rsqrt(jnp.mean(h32 * h32, axis=-1, keepdims=True) + EPS)).astype(BF16)
    values = dot_nn(normed.reshape(per * seq, width), w_value).astype(BF16)
    v3 = values.reshape(per, seq, features)
    gram_v = jnp.einsum("etf,esf->ets", v3, v3, preferred_element_type=F32)
    gram_g = jnp.einsum("etc,esc->ets", grads, grads, preferred_element_type=F32)
    totals = lax.psum(jnp.sum(gram_v * gram_g, axis=(1, 2)), "section")
    factors = clip_scale / (jnp.sqrt(totals) + GAMMA)
    weighted = (grads.astype(F32) * factors[:, None, None]).astype(BF16)
    summed = lax.psum_scatter(
        dot_tn(weighted.reshape(per * seq, width), values).astype(BF16), "dp", scatter_dimension=0, tiled=True
    )
    return summed[None]


def solution(mesh):
    in_specs = (
        P("dp", None, None), P("section", None, None), P("section", "dp", None), P("dp", None, None), P("dp"),
    )
    return jax.shard_map(
        per_device, mesh=mesh, in_specs=in_specs, out_specs=P("section", "dp", None), check_vma=False
    )
```

```python
import functools
import math

import jax
import jax.numpy as jnp
from jax import lax
from jax.experimental import pallas as pl
from jax.experimental.pallas import tpu as pltpu
from jax.sharding import PartitionSpec as P

EPS = 1e-06
GAMMA = 0.01
MESH = pl.DeviceIdType.MESH
F32 = jnp.float32
BF16 = jnp.bfloat16


def dot_nn(a, b):
    return lax.dot_general(a, b, (((1,), (0,)), ((), ())), preferred_element_type=F32)


def dot_nt(a, b):
    return lax.dot_general(a, b, (((1,), (1,)), ((), ())), preferred_element_type=F32)


def pick(cond, fn):
    def run():
        fn()

    pl.when(cond)(run)


def relay_kernel(
    cfg, inp_ref, value_ref, slice_ref, cot_ref, len_ref, out_ref,
    vbuf, wbuf, pbuf, tbuf, hbuf, obuf, gbuf, qbuf, ubuf,
    grams, cols, turned, staged, parts, scales,
    load_sem, sib_sem, ring_send, ring_recv, h_send, h_recv, g_send, g_recv,
    keep_send, keep_recv, col_send, col_recv, part_send, part_recv, scale_send, scale_recv, out_sem,
):
    secs, chips, per, width, cw, nch, tsec, clip_scale = cfg
    seq, features = hbuf.shape[1], vbuf.shape[1]
    span, own_cols = cols.shape[2], width // chips
    half_ring = chips // 2
    rows_sl = slice_ref.shape[0]
    count = 2 * per
    cn = width // nch
    sec = lax.axis_index("section")
    dp = lax.axis_index("dp")
    chip = lax.div(dp, 2)
    core = lax.rem(dp, 2)
    sib = (sec, dp + 1 - 2 * core)
    up = (sec, lax.rem(chip + 1, chips) * 2 + core)
    down = (sec, lax.rem(chip + chips - 1, chips) * 2 + core)
    nxt = (lax.rem(sec + 1, secs), dp)
    prv = (lax.rem(sec + secs - 1, secs), dp)
    first, last = sec == 0, sec == secs - 1

    barrier = pltpu.get_barrier_semaphore()

    def greet(dev):
        pl.semaphore_signal(barrier, inc=1, device_id=dev, device_id_type=MESH)

    def others(total, me, fn):
        def one(i, _):
            fn(lax.rem(me + i, total))
            return 0

        lax.fori_loop(1, total, one, 0)

    def greet_relay():
        for dev in (up, down, nxt, prv):
            greet(dev)
        pl.semaphore_wait(barrier, 5)

    def greet_helper():
        others(chips, chip, lambda i: greet((sec, 2 * i)))
        others(secs, sec, lambda i: greet((i, dp)))
        pl.semaphore_wait(barrier, chips + secs - 1)

    greet(sib)
    pick(core == 1, greet_relay)
    pick(core == 0, greet_helper)

    def remote(src, dst, send, recv, dev):
        return pltpu.make_async_remote_copy(
            src_ref=src, dst_ref=dst, send_sem=send, recv_sem=recv, device_id=dev, device_id_type=MESH
        )

    def slice_rows(index):
        return wbuf.at[pl.ds(pl.multiple_of(index * rows_sl, 16), rows_sl), :]

    def mask_rows(slot, position):
        live = lax.broadcasted_iota(jnp.int32, (seq, 1), 0) < len_ref[position]
        gbuf[slot] = jnp.where(live, gbuf[slot].astype(F32), 0.0).astype(BF16)

    def keep(src, dst, kind, mb):
        return remote(src.at[mb], dst.at[mb], keep_send.at[kind, mb], keep_recv.at[kind, mb], sib)

    def inv_rms(h32):
        return lax.rsqrt(jnp.mean(h32 * h32, axis=-1, keepdims=True) + EPS)

    def helper_core():
        to_sib = remote(slice_ref, slice_rows(2 * chip), sib_sem.at[0], sib_sem.at[1], sib)
        to_sib.start()
        load_v = pltpu.make_async_copy(value_ref, vbuf, load_sem.at[per])
        load_v.start()

        def send_inputs():
            for i in range(per):
                remote(inp_ref.at[i], hbuf.at[i], h_send.at[i], h_recv.at[i], sib).start()
            for i in range(per):
                remote(inp_ref.at[i], hbuf.at[i], h_send.at[i], h_recv.at[i], sib).wait_send()

        def send_cot():
            for i in range(per):
                pltpu.make_async_copy(cot_ref.at[i], gbuf.at[i], load_sem.at[i]).start()
            for i in range(per):
                pltpu.make_async_copy(cot_ref.at[i], gbuf.at[i], load_sem.at[i]).wait()
                mask_rows(i, i)
                remote(gbuf.at[i], gbuf.at[i], g_send.at[i], g_recv.at[i], sib).start()
            for i in range(per):
                remote(gbuf.at[i], gbuf.at[i], g_send.at[i], g_recv.at[i], sib).wait_send()

        pick(first, send_inputs)
        pick(last, send_cot)
        to_sib.wait_send()
        load_v.wait()
        block_rows = count * seq // 2
        act = pbuf.at[:, pl.ds(0, features)]

        def act_rows(index, rows=block_rows):
            return act.at[pl.ds(pl.multiple_of(index * rows, 16), rows), :]

        def make_values(mb, _):
            keep(hbuf, obuf, 0, mb).wait_recv()
            h32 = obuf[mb].astype(F32)
            normed = (h32 * inv_rms(h32)).astype(BF16)
            row = pl.multiple_of(chip * count * seq + mb * seq, 16)
            gram = jnp.zeros((seq, seq), F32)
            for c in range(2):
                cols_c = slice(c * features // 2, (c + 1) * features // 2)
                part = dot_nn(normed, vbuf[:, cols_c]).astype(BF16)
                pbuf[pl.ds(row, seq), cols_c] = part
                gram = gram + dot_nt(part, part)
            grams[mb] = gram
            return 0

        lax.fori_loop(0, count, make_values, 0)

        def ring(way, dist, half):
            step = dist - 1
            origin = lax.rem(chip + chips - step, chips) if way == 0 else lax.rem(chip + step, chips)
            block = act_rows(2 * origin + half)
            dev = up if way == 0 else down
            return remote(block, block, ring_send.at[way, step, half], ring_recv.at[way, step, half], dev)

        def arrived(way, dist, half):
            origin = lax.rem(chip + chips - dist, chips) if way == 0 else lax.rem(chip + dist, chips)
            block = act_rows(2 * origin + half)
            remote(
                block, block, ring_send.at[way, dist - 1, half], ring_recv.at[way, dist - 1, half], up
            ).wait_recv()

        for half in (1, 0):
            for way in range(2):
                ring(way, 1, half).start()

        def ring_event(e, _):
            dist, half = lax.div(e + 1, 2), lax.rem(e, 2)
            arrived(0, dist, half)
            pick(jnp.logical_or(dist + 1 < half_ring, half == 0), ring(0, dist + 1, half).start)
            arrived(1, dist, half)
            pick(jnp.logical_or(dist + 1 < half_ring, half == 1), ring(1, dist + 1, half).start)
            return 0

        lax.fori_loop(1, 2 * half_ring - 1, ring_event, 0)
        arrived(0, half_ring, 0)
        arrived(1, half_ring, 1)

        def col_start(owner):
            start = jnp.minimum(lax.div(owner * own_cols, 128) * 128, width - span)
            return pl.multiple_of(start, 128)

        def col_rows(mb):
            return pl.ds(pl.multiple_of(mb * seq, 16), seq)

        def make_parts(mb, _):
            keep(gbuf, qbuf, 1, mb).wait_recv()

            def to_owner(owner):
                remote(
                    qbuf.at[mb, :, pl.ds(col_start(owner), span)], cols.at[chip, col_rows(mb), :],
                    col_send.at[owner], col_recv.at[chip], (sec, 2 * owner),
                ).start()

            others(chips, chip, to_owner)
            cols[chip, col_rows(mb), :] = qbuf[mb, :, pl.ds(col_start(chip), span)]
            g = qbuf[mb]
            part = jnp.sum(grams[mb] * dot_nt(g, g), keepdims=True)
            parts[sec, pl.ds(mb, 1), :] = jnp.broadcast_to(part, (1, 128))
            return 0

        lax.fori_loop(0, count, make_parts, 0)

        def part_copy(to, slot):
            return remote(parts.at[slot], parts.at[slot], part_send.at[to], part_recv.at[slot], (to, dp))

        def scale_copy(to, slot):
            return remote(
                scales.at[slot], scales.at[slot], scale_send.at[to], scale_recv.at[slot], (sec, 2 * to)
            )

        others(secs, sec, lambda to: part_copy(to, sec).start())
        block = count * seq

        def col_copy(owner, source):
            return remote(cols.at[source], cols.at[source], col_send.at[owner], col_recv.at[source], sib)

        def turn(i, _):
            source = lax.rem(chip + i, chips)
            pick(i > 0, col_copy(source, source).wait_recv)
            turned[:, pl.ds(pl.multiple_of(source * block, 128), block)] = cols[source].T
            return 0

        lax.fori_loop(0, chips, turn, 0)
        others(secs, sec, lambda i: part_copy(i, i).wait_recv())
        totals = jnp.sum(parts[...], axis=0)
        scales[chip] = clip_scale / (jnp.sqrt(totals) + GAMMA)
        others(chips, chip, lambda to: scale_copy(to, chip).start())
        others(chips, chip, lambda i: scale_copy(i, i).wait_recv())
        lane = lax.broadcasted_iota(jnp.int32, (1, 128), 1)
        group = 128 // seq
        for tile in range(chips * block // 128):
            row = jnp.zeros((1, 128), F32)
            for k in range(group):
                example = tile * group + k
                value = scales[example // count, example % count:example % count + 1, :]
                row = jnp.where(lax.div(lane, seq) == k, value, row)
            at = slice(tile * 128, (tile + 1) * 128)
            turned[:, at] = (turned[:, at].astype(F32) * row).astype(BF16)

        rows_own = pl.ds(pl.multiple_of(chip * own_cols - col_start(chip), 16), own_cols)
        nout = 4
        cf = features // nout

        def out_copies(c):
            piece = pl.ds(c * cf, cf)
            near = pltpu.make_async_copy(staged.at[pl.ds(0, rows_sl), piece], out_ref.at[:, piece], out_sem.at[c])
            far = remote(
                staged.at[pl.ds(rows_sl, rows_sl), piece], out_ref.at[:, piece],
                out_sem.at[nout + c], out_sem.at[2 * nout], sib,
            )
            return near, far

        for c in range(nout):
            at = slice(c * cf, (c + 1) * cf)
            staged[:, at] = dot_nn(turned[rows_own, :], pbuf[:chips * block, at]).astype(BF16)
            for copy in out_copies(c):
                copy.start()
        for c in range(nout):
            near, far = out_copies(c)
            near.wait()
            far.wait_send()
        others(secs, sec, lambda to: part_copy(to, sec).wait_send())
        others(chips, chip, lambda to: scale_copy(to, chip).wait_send())
        others(chips, chip, lambda to: col_copy(to, chip).wait_send())
        for way in range(2):
            for dist in range(1, half_ring + 1):
                for half in range(2):
                    if dist < half_ring or half == way:
                        ring(way, dist, half).wait_send()

    def relay_core():
        load_v = pltpu.make_async_copy(value_ref, vbuf, load_sem.at[0])
        load_w = pltpu.make_async_copy(slice_ref, slice_rows(2 * chip + 1), load_sem.at[1])
        load_in = pltpu.make_async_copy(inp_ref, hbuf.at[pl.ds(per, per)], load_sem.at[2])
        load_cot = pltpu.make_async_copy(cot_ref, gbuf.at[pl.ds(per, per)], load_sem.at[3])

        def ring(way, dist, half, src=None):
            step = dist - 1
            origin = lax.rem(chip + chips - step, chips) if way == 0 else lax.rem(chip + step, chips)
            block = slice_rows(2 * origin + half)
            dev = up if way == 0 else down
            return remote(
                block if src is None else src, block,
                ring_send.at[way, step, half], ring_recv.at[way, step, half], dev,
            )

        def arrived(way, dist, half):
            origin = lax.rem(chip + chips - dist, chips) if way == 0 else lax.rem(chip + dist, chips)
            block = slice_rows(2 * origin + half)
            remote(
                block, block, ring_send.at[way, dist - 1, half], ring_recv.at[way, dist - 1, half], up
            ).wait_recv()

        for way in range(2):
            ring(way, 1, 1, slice_ref).start()
        load_w.start()
        load_v.start()
        pick(first, load_in.start)
        pick(last, load_cot.start)
        remote(slice_ref, slice_rows(2 * chip), sib_sem.at[0], sib_sem.at[1], sib).wait_recv()
        for way in range(2):
            ring(way, 1, 0).start()
        pick(first, load_in.wait)

        def ready_cot():
            load_cot.wait()
            for i in range(per):
                mask_rows(per + i, i)

        pick(last, ready_cot)
        load_w.wait()
        load_v.wait()

        def slice_event(index):
            gap = lax.rem(lax.div(index, 2) + chips - chip, chips)
            dist = jnp.minimum(gap, chips - gap)
            near = 2 * dist - lax.rem(index, 2)
            return jnp.where(dist == 0, 0, jnp.where(dist == half_ring, 2 * half_ring - 1, near))

        def chunk_event(j):
            lo, hi = lax.div(cw * j, rows_sl), lax.div(cw * j + cw - 1, rows_sl)
            event = slice_event(lo)
            for extra in range(1, cw // rows_sl + 2):
                event = jnp.maximum(event, slice_event(jnp.minimum(lo + extra, hi)))
            return event

        def make_p(event):
            def chunk(j, _):
                def run():
                    off = pl.multiple_of(j * cw, cw)
                    for m in range(nch):
                        block = dot_nt(vbuf[m * cn:(m + 1) * cn, :], wbuf[pl.ds(off, cw), :])
                        pbuf[m * cn:(m + 1) * cn, pl.ds(off, cw)] = block.astype(BF16)

                pick(chunk_event(j) == event, run)
                return 0

            lax.fori_loop(0, width // cw, chunk, 0)

        def ring_event(e, _):
            dist, half = lax.div(e + 1, 2), lax.rem(e, 2)

            def turn():
                arrived(0, dist, half)
                pick(jnp.logical_or(dist + 1 < half_ring, half == 0), ring(0, dist + 1, half).start)
                arrived(1, dist, half)
                pick(jnp.logical_or(dist + 1 < half_ring, half == 1), ring(1, dist + 1, half).start)

            def final():
                arrived(0, half_ring, 0)
                arrived(1, half_ring, 1)

            pick(jnp.logical_and(e > 0, e < 2 * half_ring - 1), turn)
            pick(e == 2 * half_ring - 1, final)
            make_p(e)
            return 0

        lax.fori_loop(0, 2 * half_ring, ring_event, 0)

        def make_t():
            def chunk(j, _):
                off = pl.multiple_of(j * cw, cw)
                for m in range(nch):
                    block = dot_nt(wbuf[pl.ds(off, cw), :], vbuf[m * cn:(m + 1) * cn, :])
                    tbuf[pl.ds(off, cw), m * cn:(m + 1) * cn] = block.astype(BF16)
                return 0

            lax.fori_loop(0, width // cw, chunk, 0)

        pick(sec >= tsec, make_t)

        def whole(buf, mb, send, recv, dev):
            return remote(buf.at[mb], buf.at[mb], send.at[mb], recv.at[mb], dev)

        def forward(mb, _):
            pick(jnp.logical_or(sec > 0, mb < per), whole(hbuf, mb, h_send, h_recv, sib).wait_recv)
            keep(hbuf, obuf, 0, mb).start()
            h = hbuf[mb]
            h32 = h.astype(F32)
            r = inv_rms(h32)
            for c in range(nch):
                cols = pl.ds(c * cn, cn)
                u = dot_nn(h, pbuf[:width, c * cn:(c + 1) * cn])
                ubuf[mb, :, c * cn:(c + 1) * cn] = u
                obuf[mb, :, c * cn:(c + 1) * cn] = (h32[:, c * cn:(c + 1) * cn] + r * u).astype(BF16)
                remote(
                    obuf.at[mb, :, cols], hbuf.at[mb, :, cols], h_send.at[mb], h_recv.at[mb], nxt
                ).start()
            return 0

        pick(sec < secs - 1, lambda: lax.fori_loop(0, count, forward, 0))
        pick(jnp.logical_and(sec > 0, sec < tsec), make_t)

        def send_grad(mb, c):
            cols = pl.ds(c * cn, cn)
            remote(
                qbuf.at[mb, :, cols], gbuf.at[mb, :, cols], g_send.at[mb], g_recv.at[mb], prv
            ).start()

        def backward(mb, _):
            whole(gbuf, mb, g_send, g_recv, sib).wait_recv()
            keep(gbuf, qbuf, 1, mb).start()
            g = gbuf[mb]
            g32, h32 = g.astype(F32), hbuf[mb].astype(F32)
            r = inv_rms(h32)
            coef = jnp.sum(g32 * ubuf[mb], axis=-1, keepdims=True) * (r * r * r) * (1.0 / width)
            for c in range(nch):
                lo, hi = c * cn, (c + 1) * cn
                p = dot_nn(g, tbuf[:, lo:hi])
                qbuf[mb, :, lo:hi] = (g32[:, lo:hi] + r * p - coef * h32[:, lo:hi]).astype(BF16)
                send_grad(mb, c)
            return 0

        def backward_last(mb, _):
            pick(mb < per, whole(gbuf, mb, g_send, g_recv, sib).wait_recv)
            keep(gbuf, qbuf, 1, mb).start()
            whole(hbuf, mb, h_send, h_recv, sib).wait_recv()
            keep(hbuf, obuf, 0, mb).start()
            g = gbuf[mb]
            g32, h32 = g.astype(F32), hbuf[mb].astype(F32)
            r = inv_rms(h32)
            dots = jnp.zeros_like(r)
            for c in range(nch):
                lo, hi = c * cn, (c + 1) * cn
                p = dot_nn(g, tbuf[:, lo:hi])
                ubuf[mb, :, lo:hi] = p
                dots = dots + jnp.sum(p * h32[:, lo:hi], axis=-1, keepdims=True)
            coef = dots * (r * r * r) * (1.0 / width)
            for c in range(nch):
                lo, hi = c * cn, (c + 1) * cn
                p = ubuf[mb, :, lo:hi]
                qbuf[mb, :, lo:hi] = (g32[:, lo:hi] + r * p - coef * h32[:, lo:hi]).astype(BF16)
                send_grad(mb, c)
            return 0

        def backward_first(mb, _):
            whole(gbuf, mb, g_send, g_recv, sib).wait_recv()
            keep(gbuf, qbuf, 1, mb).start()
            return 0

        pick(last, lambda: lax.fori_loop(0, count, backward_last, 0))
        pick(
            jnp.logical_and(sec > 0, sec < secs - 1),
            lambda: lax.fori_loop(0, count, backward, 0),
        )
        pick(first, lambda: lax.fori_loop(0, count, backward_first, 0))

        def drain(mb, _):
            pick(sec < secs - 1, whole(hbuf, mb, h_send, h_recv, nxt).wait_send)
            pick(sec > 0, whole(gbuf, mb, g_send, g_recv, prv).wait_send)
            keep(hbuf, obuf, 0, mb).wait_send()
            keep(gbuf, qbuf, 1, mb).wait_send()
            return 0

        lax.fori_loop(0, count, drain, 0)
        for way in range(2):
            for dist in range(1, half_ring + 1):
                for half in range(2):
                    if dist < half_ring or half == way:
                        ring(way, dist, half).wait_send()
        remote(out_ref, out_ref, out_sem.at[0], out_sem.at[out_sem.shape[0] - 1], sib).wait_recv()

    pick(core == 0, helper_core)
    pick(core == 1, relay_core)


def per_device(inputs, value_weight, output_weight, cotangent, lengths, cw=256, nch=3, tsec=10):
    per, seq, width = inputs.shape
    features = value_weight.shape[2]
    rows_sl = output_weight.shape[1]
    secs, chips = lax.axis_size("section"), lax.axis_size("dp") // 2
    count = 2 * per
    own = width // chips
    span = max(-(-(i * own + own) // 128) - (i * own) // 128 for i in range(chips)) * 128
    clip_scale = math.sqrt(features * width * 1.0 / (count * chips))
    any_spec = pl.BlockSpec(memory_space=pl.ANY)
    dma = pltpu.SemaphoreType.DMA
    tall, wide = max(width, chips * count * seq), max(width, features)
    result = pl.pallas_call(
        functools.partial(relay_kernel, (secs, chips, per, width, cw, nch, tsec, clip_scale)),
        out_shape=jax.ShapeDtypeStruct((rows_sl, features), BF16),
        in_specs=[any_spec] * 4 + [pl.BlockSpec(memory_space=pltpu.SMEM)],
        out_specs=any_spec,
        scratch_shapes=[
            pltpu.VMEM((width, features), BF16),
            pltpu.VMEM((width, features), BF16),
            pltpu.VMEM((tall, wide), BF16),
            pltpu.VMEM((width, width), BF16),
            pltpu.VMEM((count, seq, width), BF16),
            pltpu.VMEM((count, seq, width), BF16),
            pltpu.VMEM((count, seq, width), BF16),
            pltpu.VMEM((count, seq, width), BF16),
            pltpu.VMEM((count, seq, width), F32),
            pltpu.VMEM((count, seq, seq), F32),
            pltpu.VMEM((chips, count * seq, span), BF16),
            pltpu.VMEM((span, chips * count * seq), BF16),
            pltpu.VMEM((own, features), BF16),
            pltpu.VMEM((secs, count, 128), F32),
            pltpu.VMEM((chips, count, 128), F32),
            dma((per + 4,)),
            dma((2,)),
            dma((2, chips // 2, 2)),
            dma((2, chips // 2, 2)),
            dma((count,)),
            dma((count,)),
            dma((count,)),
            dma((count,)),
            dma((2, count)),
            dma((2, count)),
            dma((chips,)),
            dma((chips,)),
            dma((secs,)),
            dma((secs,)),
            dma((chips,)),
            dma((chips,)),
            dma((9,)),
        ],
        compiler_params=pltpu.CompilerParams(
            collective_id=0, has_side_effects=True, vmem_limit_bytes=60 << 20
        ),
    )(inputs, value_weight[0], output_weight[0], cotangent, lengths)
    return result[None]


def solution(mesh):
    in_specs = (
        P("dp", None, None), P("section", None, None), P("section", "dp", None), P("dp", None, None), P("dp"),
    )
    return jax.shard_map(
        per_device, mesh=mesh, in_specs=in_specs, out_specs=P("section", "dp", None), check_vma=False
    )
```

```python
import functools
import math

import jax
import jax.numpy as jnp
from jax import lax
from jax.experimental import pallas as pl
from jax.experimental.pallas import tpu as pltpu
from jax.sharding import PartitionSpec as P

EPS = 1e-06
GAMMA = 0.01
MESH = pl.DeviceIdType.MESH
CUTS = (0, 1280, 2304)
F32 = jnp.float32
BF16 = jnp.bfloat16


def dot_nn(a, b):
    return lax.dot_general(a, b, (((1,), (0,)), ((), ())), preferred_element_type=F32)


def dot_nt(a, b):
    return lax.dot_general(a, b, (((1,), (1,)), ((), ())), preferred_element_type=F32)


def dot_tall(a, b):
    rows = a.shape[0]
    tall = jnp.concatenate([a] * (128 // rows), axis=0)
    return dot_nn(tall, b)[:rows]


def pick(cond, fn):
    def run():
        fn()

    pl.when(cond)(run)


def relay_kernel(
    cfg, inp_ref, value_ref, slice_ref, cot_ref, len_ref, out_ref,
    vbuf, wbuf, pbuf, tbuf, hbuf, obuf, gbuf, qbuf, ubuf,
    grams, cols, turned, staged, parts, scales,
    load_sem, sib_sem, ring_send, ring_recv, h_send, h_recv, g_send, g_recv,
    keep_send, keep_recv, col_send, col_recv, part_send, part_recv, scale_send, scale_recv, out_sem,
):
    secs, chips, per, width, cw, nch, tsec, cuts, clip_scale = cfg
    seq, features = hbuf.shape[1], vbuf.shape[1]
    span, own_cols = cols.shape[2], width // chips
    half_ring = chips // 2
    rows_sl = slice_ref.shape[0]
    pieces = 3
    rows_pc = rows_sl // pieces
    count = 2 * per
    cn = width // nch
    sec = lax.axis_index("section")
    dp = lax.axis_index("dp")
    chip = lax.div(dp, 2)
    core = lax.rem(dp, 2)
    sib = (sec, dp + 1 - 2 * core)
    up = (sec, lax.rem(chip + 1, chips) * 2 + core)
    down = (sec, lax.rem(chip + chips - 1, chips) * 2 + core)
    nxt = (lax.rem(sec + 1, secs), dp)
    prv = (lax.rem(sec + secs - 1, secs), dp)
    first, last = sec == 0, sec == secs - 1

    part_rows = width // 4

    def load_values(wait):
        for i in range(4):
            rows = pl.ds(i * part_rows, part_rows)
            copy = pltpu.make_async_copy(value_ref.at[rows, :], vbuf.at[rows, :], load_sem.at[per + i])
            copy.wait() if wait else copy.start()

    load_values(wait=False)
    barrier = pltpu.get_barrier_semaphore()

    def greet(dev):
        pl.semaphore_signal(barrier, inc=1, device_id=dev, device_id_type=MESH)

    def others(total, me, fn):
        if total == 16:
            far = (0, 1, 2, 1)
            steps = sorted(range(1, 16), key=lambda i: -far[i // 4] - far[i % 4])
            for i in steps:
                row, col = lax.rem(lax.div(me, 4) + i // 4, 4), lax.rem(lax.rem(me, 4) + i % 4, 4)
                fn(row * 4 + col)
        else:
            for i in sorted(range(1, total), key=lambda i: -min(i, total - i)):
                fn(lax.rem(me + i, total))

    def greet_relay():
        for dev in (up, down, nxt, prv, sib):
            greet(dev)
        pl.semaphore_wait(barrier, 4)

    pick(core == 1, greet_relay)
    pick(core == 0, lambda: pl.semaphore_wait(barrier, 1))

    def remote(src, dst, send, recv, dev):
        return pltpu.make_async_remote_copy(
            src_ref=src, dst_ref=dst, send_sem=send, recv_sem=recv, device_id=dev, device_id_type=MESH
        )

    def slice_rows(index):
        return wbuf.at[pl.ds(pl.multiple_of(index * rows_sl, 16), rows_sl), :]

    def mask_rows(slot, position):
        live = lax.broadcasted_iota(jnp.int32, (seq, 1), 0) < len_ref[position]
        gbuf[slot] = jnp.where(live, gbuf[slot].astype(F32), 0.0).astype(BF16)

    def keep(src, dst, kind, mb):
        return remote(src.at[mb], dst.at[mb], keep_send.at[kind, mb], keep_recv.at[kind, mb], sib)

    def inv_rms(h32):
        return lax.rsqrt(jnp.mean(h32 * h32, axis=-1, keepdims=True) + EPS)

    def helper_core():
        to_sib = remote(slice_ref, slice_rows(2 * chip), sib_sem.at[0], sib_sem.at[1], sib)
        to_sib.start()
        def send_inputs():
            for i in range(per):
                remote(inp_ref.at[i], hbuf.at[i], h_send.at[i], h_recv.at[i], sib).start()
            for i in range(per):
                remote(inp_ref.at[i], hbuf.at[i], h_send.at[i], h_recv.at[i], sib).wait_send()

        def send_cot():
            for i in range(per):
                pltpu.make_async_copy(cot_ref.at[i], gbuf.at[i], load_sem.at[i]).start()
            for i in range(per):
                pltpu.make_async_copy(cot_ref.at[i], gbuf.at[i], load_sem.at[i]).wait()
                mask_rows(i, i)
                remote(gbuf.at[i], gbuf.at[i], g_send.at[i], g_recv.at[i], sib).start()
            for i in range(per):
                remote(gbuf.at[i], gbuf.at[i], g_send.at[i], g_recv.at[i], sib).wait_send()

        pick(first, send_inputs)
        pick(last, send_cot)
        to_sib.wait_send()
        load_values(wait=True)
        block_rows = count * seq // 2
        act = pbuf.at[:, pl.ds(0, features)]

        def act_rows(index, rows=block_rows):
            return act.at[pl.ds(pl.multiple_of(index * rows, 16), rows), :]

        def make_values(mb, _):
            keep(hbuf, obuf, 0, mb).wait_recv()
            h32 = obuf[mb].astype(F32)
            normed = (h32 * inv_rms(h32)).astype(BF16)
            row = pl.multiple_of(chip * count * seq + mb * seq, 16)
            gram = jnp.zeros((seq, seq), F32)
            for c in range(2):
                cols_c = slice(c * features // 2, (c + 1) * features // 2)
                part = dot_nn(normed, vbuf[:, cols_c]).astype(BF16)
                pbuf[pl.ds(row, seq), cols_c] = part
                gram = gram + dot_nt(part, part)
            grams[mb] = gram
            return 0

        lax.fori_loop(0, count, make_values, 0)

        def ring(way, dist, half):
            step = dist - 1
            origin = lax.rem(chip + chips - step, chips) if way == 0 else lax.rem(chip + step, chips)
            block = act_rows(2 * origin + half)
            dev = up if way == 0 else down
            return remote(block, block, ring_send.at[way, step, half], ring_recv.at[way, step, half], dev)

        def arrived(way, dist, half):
            origin = lax.rem(chip + chips - dist, chips) if way == 0 else lax.rem(chip + dist, chips)
            block = act_rows(2 * origin + half)
            remote(
                block, block, ring_send.at[way, dist - 1, half], ring_recv.at[way, dist - 1, half], up
            ).wait_recv()

        for way in range(2):
            ring(way, 1, 1).start()
        for way in range(2):
            ring(way, 1, 1).wait_send()
            ring(way, 1, 0).start()

        def ring_event(e, _):
            dist, half = lax.div(e + 1, 2), lax.rem(e, 2)
            arrived(0, dist, half)
            pick(jnp.logical_or(dist + 1 < half_ring, half == 0), ring(0, dist + 1, half).start)
            arrived(1, dist, half)
            pick(jnp.logical_or(dist + 1 < half_ring, half == 1), ring(1, dist + 1, half).start)
            return 0

        lax.fori_loop(1, 2 * half_ring - 1, ring_event, 0)
        arrived(0, half_ring, 0)
        arrived(1, half_ring, 1)

        def col_start(owner):
            start = jnp.minimum(lax.div(owner * own_cols, 128) * 128, width - span)
            return pl.multiple_of(start, 128)

        def col_rows(mb):
            return pl.ds(pl.multiple_of(mb * seq, 16), seq)

        def make_parts(mb, _):
            keep(gbuf, qbuf, 1, mb).wait_recv()

            def to_owner(owner):
                remote(
                    qbuf.at[mb, :, pl.ds(col_start(owner), span)], cols.at[chip, col_rows(mb), :],
                    col_send.at[owner], col_recv.at[chip], (sec, 2 * owner),
                ).start()

            others(chips, chip, to_owner)
            cols[chip, col_rows(mb), :] = qbuf[mb, :, pl.ds(col_start(chip), span)]
            g = qbuf[mb]
            part = jnp.sum(grams[mb] * dot_nt(g, g), keepdims=True)
            parts[sec, pl.ds(mb, 1), :] = jnp.broadcast_to(part, (1, 128))
            return 0

        lax.fori_loop(0, count, make_parts, 0)

        def part_copy(to, slot):
            return remote(parts.at[slot], parts.at[slot], part_send.at[to], part_recv.at[slot], (to, dp))

        def scale_copy(to, slot):
            return remote(
                scales.at[slot], scales.at[slot], scale_send.at[to], scale_recv.at[slot], (sec, 2 * to)
            )

        others(secs, sec, lambda to: part_copy(to, sec).start())
        block = count * seq

        def col_copy(owner, source):
            return remote(cols.at[source], cols.at[source], col_send.at[owner], col_recv.at[source], sib)

        def turn(i, _):
            source = lax.rem(chip + i, chips)
            pick(i > 0, col_copy(source, source).wait_recv)
            turned[:, pl.ds(pl.multiple_of(source * block, 128), block)] = cols[source].T
            return 0

        lax.fori_loop(0, chips, turn, 0)
        others(secs, sec, lambda i: part_copy(i, i).wait_recv())
        totals = jnp.sum(parts[...], axis=0)
        scales[chip] = clip_scale / (jnp.sqrt(totals) + GAMMA)
        others(chips, chip, lambda to: scale_copy(to, chip).start())
        others(chips, chip, lambda i: scale_copy(i, i).wait_recv())
        lane = lax.broadcasted_iota(jnp.int32, (1, 128), 1)
        group = 128 // seq
        for tile in range(chips * block // 128):
            row = jnp.zeros((1, 128), F32)
            for k in range(group):
                example = tile * group + k
                value = scales[example // count, example % count:example % count + 1, :]
                row = jnp.where(lax.div(lane, seq) == k, value, row)
            at = slice(tile * 128, (tile + 1) * 128)
            turned[:, at] = (turned[:, at].astype(F32) * row).astype(BF16)

        rows_own = pl.ds(pl.multiple_of(chip * own_cols - col_start(chip), 16), own_cols)
        nout = 4
        cf = features // nout

        def out_copies(c):
            piece = pl.ds(c * cf, cf)
            near = pltpu.make_async_copy(staged.at[pl.ds(0, rows_sl), piece], out_ref.at[:, piece], out_sem.at[c])
            far = remote(
                staged.at[pl.ds(rows_sl, rows_sl), piece], out_ref.at[:, piece],
                out_sem.at[nout + c], out_sem.at[2 * nout], sib,
            )
            return near, far

        for c in range(nout):
            at = slice(c * cf, (c + 1) * cf)
            staged[:, at] = dot_nn(turned[rows_own, :], pbuf[:chips * block, at]).astype(BF16)
            for copy in out_copies(c):
                copy.start()
        for c in range(nout):
            near, far = out_copies(c)
            near.wait()
            far.wait_send()
        others(secs, sec, lambda to: part_copy(to, sec).wait_send())
        others(chips, chip, lambda to: scale_copy(to, chip).wait_send())
        others(chips, chip, lambda to: col_copy(to, chip).wait_send())
        for way in range(2):
            for dist in range(1, half_ring + 1):
                for half in range(2):
                    if (dist < half_ring or half == way) and (dist, half) != (1, 1):
                        ring(way, dist, half).wait_send()

    def relay_core():
        load_w = pltpu.make_async_copy(slice_ref, slice_rows(2 * chip + 1), load_sem.at[0])
        load_in = pltpu.make_async_copy(inp_ref, hbuf.at[pl.ds(per, per)], load_sem.at[1])
        load_cot = pltpu.make_async_copy(cot_ref, gbuf.at[pl.ds(per, per)], load_sem.at[2])
        load_w.start()
        pick(first, load_in.start)
        pick(last, load_cot.start)
        turns = 2 * pieces

        def piece_rows(origin, order):
            index = origin * turns + lax.rem(order + pieces, turns)
            return wbuf.at[pl.ds(pl.multiple_of(index * rows_pc, 16), rows_pc), :]

        def ring(way, dist, order, src=None):
            step = dist - 1
            origin = lax.rem(chip + chips - step, chips) if way == 0 else lax.rem(chip + step, chips)
            block = piece_rows(origin, order)
            dev = up if way == 0 else down
            return remote(
                block if src is None else src, block,
                ring_send.at[way, step, order], ring_recv.at[way, step, order], dev,
            )

        def arrived(way, dist, order):
            origin = lax.rem(chip + chips - dist, chips) if way == 0 else lax.rem(chip + dist, chips)
            block = piece_rows(origin, order)
            remote(
                block, block, ring_send.at[way, dist - 1, order], ring_recv.at[way, dist - 1, order], up
            ).wait_recv()

        for order in range(turns):
            if order == pieces:
                remote(slice_ref, slice_rows(2 * chip), sib_sem.at[0], sib_sem.at[1], sib).wait_recv()
            src = slice_ref.at[pl.ds(order * rows_pc, rows_pc), :] if order < pieces else None
            for way in range(2):
                if order >= pieces:
                    ring(way, 1, order - pieces).wait_send()
                ring(way, 1, order, src).start()
        pick(first, load_in.wait)

        def ready_cot():
            load_cot.wait()
            for i in range(per):
                mask_rows(per + i, i)

        pick(last, ready_cot)
        load_w.wait()
        load_values(wait=True)
        chunks = width // cw

        def chip_gap(index):
            gap = lax.rem(index + chips - chip, chips)
            return jnp.minimum(gap, chips - gap)

        def chunk_level(j):
            rows = 2 * rows_sl
            level = chip_gap(lax.div(cw * j, rows))
            for extra in range(1, (cw - 2) // rows + 2):
                level = jnp.maximum(level, chip_gap(lax.div(jnp.minimum(cw * j + extra * rows, cw * j + cw - 1), rows)))
            return level

        def make_p(level, start, number):
            def chunk(j, _):
                def run():
                    off = pl.multiple_of(j * cw, cw)
                    for m in range(nch):
                        block = dot_nt(vbuf[m * cn:(m + 1) * cn, :], wbuf[pl.ds(off, cw), :])
                        pbuf[m * cn:(m + 1) * cn, pl.ds(off, cw)] = block.astype(BF16)

                pick(jnp.logical_and(j < chunks, chunk_level(jnp.minimum(j, chunks - 1)) == level), run)
                return 0

            lax.fori_loop(start, start + number, chunk, 0)

        def ring_event(e, _):
            dist, order = lax.div(e, turns) + 1, lax.rem(e, turns)
            arrived(0, dist, order)
            pick(jnp.logical_or(dist + 1 < half_ring, order < pieces), ring(0, dist + 1, order).start)
            arrived(1, dist, order)
            pick(jnp.logical_or(dist + 1 < half_ring, order >= pieces), ring(1, dist + 1, order).start)
            each = -(-chunks // turns)
            make_p(dist - 1, order * each, each)
            return 0

        lax.fori_loop(0, (half_ring - 1) * turns, ring_event, 0)

        def final_event(k, _):
            arrived(0, half_ring, k)
            arrived(1, half_ring, k + pieces)
            each = -(-chunks // pieces)
            make_p(half_ring - 1, k * each, each)
            return 0

        lax.fori_loop(0, pieces, final_event, 0)
        make_p(half_ring, 0, chunks)

        def make_t():
            def chunk(j, _):
                off = pl.multiple_of(j * cw, cw)
                for m in range(nch):
                    block = dot_nt(wbuf[pl.ds(off, cw), :], vbuf[m * cn:(m + 1) * cn, :])
                    tbuf[pl.ds(off, cw), m * cn:(m + 1) * cn] = block.astype(BF16)
                return 0

            lax.fori_loop(0, width // cw, chunk, 0)

        pick(sec >= tsec, make_t)

        def whole(buf, mb, send, recv, dev):
            return remote(buf.at[mb], buf.at[mb], send.at[mb], recv.at[mb], dev)

        def forward(mb, _):
            pick(jnp.logical_or(sec > 0, mb < per), whole(hbuf, mb, h_send, h_recv, sib).wait_recv)
            h = hbuf[mb]
            h32 = h.astype(F32)
            r = inv_rms(h32)
            for lo, hi in zip(cuts, cuts[1:]):
                piece = pl.ds(lo, hi - lo)
                u = dot_tall(h, pbuf[:width, lo:hi])
                ubuf[mb, :, lo:hi] = u
                obuf[mb, :, lo:hi] = (h32[:, lo:hi] + r * u).astype(BF16)
                remote(
                    obuf.at[mb, :, piece], hbuf.at[mb, :, piece], h_send.at[mb], h_recv.at[mb], nxt
                ).start()
            keep(hbuf, obuf, 0, mb).start()
            return 0

        pick(sec < secs - 1, lambda: lax.fori_loop(0, count, forward, 0))
        pick(jnp.logical_and(sec > 0, sec < tsec), make_t)

        def send_grad(mb, lo, hi):
            piece = pl.ds(lo, hi - lo)
            remote(
                qbuf.at[mb, :, piece], gbuf.at[mb, :, piece], g_send.at[mb], g_recv.at[mb], prv
            ).start()

        def backward(batch, step, _):
            at = pl.ds(step * batch, batch)
            for i in range(batch):
                whole(gbuf, step * batch + i, g_send, g_recv, sib).wait_recv()
            rows = batch * seq
            g = gbuf[at].reshape(rows, width)
            g32, h32 = g.astype(F32), hbuf[at].reshape(rows, width).astype(F32)
            r = inv_rms(h32)
            coef = jnp.sum(g32 * ubuf[at].reshape(rows, width), axis=-1, keepdims=True) * (r * r * r) * (1.0 / width)
            for lo, hi in zip(cuts, cuts[1:]):
                p = dot_tall(g, tbuf[:, lo:hi])
                result = (g32[:, lo:hi] + r * p - coef * h32[:, lo:hi]).astype(BF16)
                qbuf[at, :, lo:hi] = result.reshape(batch, seq, hi - lo)
                for i in range(batch):
                    send_grad(step * batch + i, lo, hi)
            for i in range(batch):
                keep(gbuf, qbuf, 1, step * batch + i).start()
            return 0

        def backward_last(mb, _):
            pick(mb < per, whole(gbuf, mb, g_send, g_recv, sib).wait_recv)
            keep(gbuf, qbuf, 1, mb).start()
            whole(hbuf, mb, h_send, h_recv, sib).wait_recv()
            keep(hbuf, obuf, 0, mb).start()
            g = gbuf[mb]
            g32, h32 = g.astype(F32), hbuf[mb].astype(F32)
            r = inv_rms(h32)
            dots = jnp.zeros_like(r)
            for lo, hi in zip(cuts, cuts[1:]):
                p = dot_tall(g, tbuf[:, lo:hi])
                ubuf[mb, :, lo:hi] = p
                dots = dots + jnp.sum(p * h32[:, lo:hi], axis=-1, keepdims=True)
            coef = dots * (r * r * r) * (1.0 / width)
            for lo, hi in zip(cuts, cuts[1:]):
                p = ubuf[mb, :, lo:hi]
                qbuf[mb, :, lo:hi] = (g32[:, lo:hi] + r * p - coef * h32[:, lo:hi]).astype(BF16)
                send_grad(mb, lo, hi)
            return 0

        def backward_first(mb, _):
            whole(gbuf, mb, g_send, g_recv, sib).wait_recv()
            keep(gbuf, qbuf, 1, mb).start()
            return 0

        pick(last, lambda: lax.fori_loop(0, count, backward_last, 0))
        pick(
            jnp.logical_and(sec > 0, sec < secs - 2),
            lambda: lax.fori_loop(0, count, functools.partial(backward, 1), 0),
        )
        pick(
            jnp.logical_and(sec > 0, sec == secs - 2),
            lambda: lax.fori_loop(0, count // 2, functools.partial(backward, 2), 0),
        )
        pick(first, lambda: lax.fori_loop(0, count, backward_first, 0))

        def drain(mb, _):
            pick(sec < secs - 1, whole(hbuf, mb, h_send, h_recv, nxt).wait_send)
            pick(sec > 0, whole(gbuf, mb, g_send, g_recv, prv).wait_send)
            keep(hbuf, obuf, 0, mb).wait_send()
            keep(gbuf, qbuf, 1, mb).wait_send()
            return 0

        lax.fori_loop(0, count, drain, 0)
        for way in range(2):
            for dist in range(1, half_ring + 1):
                for order in range(turns):
                    if dist == half_ring and (order < pieces) != (way == 0):
                        continue
                    if dist > 1 or order >= pieces:
                        ring(way, dist, order).wait_send()
        remote(out_ref, out_ref, out_sem.at[0], out_sem.at[out_sem.shape[0] - 1], sib).wait_recv()

    pick(core == 0, helper_core)
    pick(core == 1, relay_core)


def per_device(inputs, value_weight, output_weight, cotangent, lengths, cw=256, nch=3, tsec=10, cuts=CUTS):
    per, seq, width = inputs.shape
    features = value_weight.shape[2]
    rows_sl = output_weight.shape[1]
    secs, chips = lax.axis_size("section"), lax.axis_size("dp") // 2
    count = 2 * per
    own = width // chips
    span = max(-(-(i * own + own) // 128) - (i * own) // 128 for i in range(chips)) * 128
    clip_scale = math.sqrt(features * width * 1.0 / (count * chips))
    any_spec = pl.BlockSpec(memory_space=pl.ANY)
    dma = pltpu.SemaphoreType.DMA
    tall, wide = max(width, chips * count * seq), max(width, features)
    result = pl.pallas_call(
        functools.partial(relay_kernel, (secs, chips, per, width, cw, nch, tsec, cuts, clip_scale)),
        out_shape=jax.ShapeDtypeStruct((rows_sl, features), BF16),
        in_specs=[any_spec] * 4 + [pl.BlockSpec(memory_space=pltpu.SMEM)],
        out_specs=any_spec,
        scratch_shapes=[
            pltpu.VMEM((width, features), BF16),
            pltpu.VMEM((width, features), BF16),
            pltpu.VMEM((tall, wide), BF16),
            pltpu.VMEM((width, width), BF16),
            pltpu.VMEM((count, seq, width), BF16),
            pltpu.VMEM((count, seq, width), BF16),
            pltpu.VMEM((count, seq, width), BF16),
            pltpu.VMEM((count, seq, width), BF16),
            pltpu.VMEM((count, seq, width), F32),
            pltpu.VMEM((count, seq, seq), F32),
            pltpu.VMEM((chips, count * seq, span), BF16),
            pltpu.VMEM((span, chips * count * seq), BF16),
            pltpu.VMEM((own, features), BF16),
            pltpu.VMEM((secs, count, 128), F32),
            pltpu.VMEM((chips, count, 128), F32),
            dma((per + 7,)),
            dma((2,)),
            dma((2, chips // 2, 6)),
            dma((2, chips // 2, 6)),
            dma((count,)),
            dma((count,)),
            dma((count,)),
            dma((count,)),
            dma((2, count)),
            dma((2, count)),
            dma((chips,)),
            dma((chips,)),
            dma((secs,)),
            dma((secs,)),
            dma((chips,)),
            dma((chips,)),
            dma((9,)),
        ],
        compiler_params=pltpu.CompilerParams(
            collective_id=0, has_side_effects=True, vmem_limit_bytes=60 << 20
        ),
    )(inputs, value_weight[0], output_weight[0], cotangent, lengths)
    return result[None]


def solution(mesh):
    in_specs = (
        P("dp", None, None), P("section", None, None), P("section", "dp", None), P("dp", None, None), P("dp"),
    )
    return jax.shard_map(
        per_device, mesh=mesh, in_specs=in_specs, out_specs=P("section", "dp", None), check_vma=False
    )
```

```python
import functools
import math

import jax
import jax.numpy as jnp
from jax import lax
from jax.experimental import pallas as pl
from jax.experimental.pallas import tpu as pltpu
from jax.sharding import PartitionSpec as P

EPS = 1e-06
GAMMA = 0.01
MESH = pl.DeviceIdType.MESH
CUTS = (0, 1280, 2304)
F32 = jnp.float32
BF16 = jnp.bfloat16


def dot_nn(a, b):
    return lax.dot_general(a, b, (((1,), (0,)), ((), ())), preferred_element_type=F32)


def dot_nt(a, b):
    return lax.dot_general(a, b, (((1,), (1,)), ((), ())), preferred_element_type=F32)


def dot_tall(a, b):
    rows = a.shape[0]
    tall = jnp.concatenate([a] * (128 // rows), axis=0)
    return dot_nn(tall, b)[:rows]


def pick(cond, fn):
    def run():
        fn()

    pl.when(cond)(run)


def relay_kernel(
    cfg, inp_ref, value_ref, slice_ref, cot_ref, len_ref, out_ref,
    vbuf, wbuf, pbuf, tbuf, hbuf, obuf, gbuf, qbuf, ubuf,
    grams, cols, turned, staged, parts, scales,
    load_sem, sib_sem, ring_send, ring_recv, h_send, h_recv, g_send, g_recv,
    keep_send, keep_recv, col_send, col_recv, part_send, part_recv, scale_send, scale_recv, out_sem,
):
    secs, chips, per, width, cw, nch, tsec, cuts, clip_scale = cfg
    seq, features = hbuf.shape[1], vbuf.shape[1]
    span, own_cols = cols.shape[2], width // chips
    half_ring = chips // 2
    rows_sl = slice_ref.shape[0]
    pieces = 3
    rows_pc = rows_sl // pieces
    count = 2 * per
    cn = width // nch
    sec = lax.axis_index("section")
    dp = lax.axis_index("dp")
    chip = lax.div(dp, 2)
    core = lax.rem(dp, 2)
    sib = (sec, dp + 1 - 2 * core)
    up = (sec, lax.rem(chip + 1, chips) * 2 + core)
    down = (sec, lax.rem(chip + chips - 1, chips) * 2 + core)
    nxt = (lax.rem(sec + 1, secs), dp)
    prv = (lax.rem(sec + secs - 1, secs), dp)
    first, last = sec == 0, sec == secs - 1

    part_rows = width // 4

    def load_values(wait):
        for i in range(4):
            rows = pl.ds(i * part_rows, part_rows)
            copy = pltpu.make_async_copy(value_ref.at[rows, :], vbuf.at[rows, :], load_sem.at[per + i])
            copy.wait() if wait else copy.start()

    load_values(wait=False)
    barrier = pltpu.get_barrier_semaphore()

    def greet(dev):
        pl.semaphore_signal(barrier, inc=1, device_id=dev, device_id_type=MESH)

    def others(total, me, fn):
        if total == 16:
            far = (0, 1, 2, 1)
            steps = sorted(range(1, 16), key=lambda i: -far[i // 4] - far[i % 4])
            for i in steps:
                row, col = lax.rem(lax.div(me, 4) + i // 4, 4), lax.rem(lax.rem(me, 4) + i % 4, 4)
                fn(row * 4 + col)
        else:
            for i in sorted(range(1, total), key=lambda i: -min(i, total - i)):
                fn(lax.rem(me + i, total))

    def greet_relay():
        for dev in (up, down, nxt, prv, sib):
            greet(dev)
        pl.semaphore_wait(barrier, 4)

    pick(core == 1, greet_relay)
    pick(core == 0, lambda: pl.semaphore_wait(barrier, 1))

    def remote(src, dst, send, recv, dev):
        return pltpu.make_async_remote_copy(
            src_ref=src, dst_ref=dst, send_sem=send, recv_sem=recv, device_id=dev, device_id_type=MESH
        )

    def slice_rows(index):
        return wbuf.at[pl.ds(pl.multiple_of(index * rows_sl, 16), rows_sl), :]

    def mask_rows(slot, position):
        live = lax.broadcasted_iota(jnp.int32, (seq, 1), 0) < len_ref[position]
        gbuf[slot] = jnp.where(live, gbuf[slot].astype(F32), 0.0).astype(BF16)

    def keep(src, dst, kind, mb):
        return remote(src.at[mb], dst.at[mb], keep_send.at[kind, mb], keep_recv.at[kind, mb], sib)

    def inv_rms(h32):
        return lax.rsqrt(jnp.mean(h32 * h32, axis=-1, keepdims=True) + EPS)

    def helper_core():
        to_sib = remote(slice_ref, slice_rows(2 * chip), sib_sem.at[0], sib_sem.at[1], sib)
        to_sib.start()
        def send_inputs():
            for i in range(per):
                remote(inp_ref.at[i], hbuf.at[i], h_send.at[i], h_recv.at[i], sib).start()
            for i in range(per):
                remote(inp_ref.at[i], hbuf.at[i], h_send.at[i], h_recv.at[i], sib).wait_send()

        def send_cot():
            for i in range(per):
                pltpu.make_async_copy(cot_ref.at[i], gbuf.at[i], load_sem.at[i]).start()
            for i in range(per):
                pltpu.make_async_copy(cot_ref.at[i], gbuf.at[i], load_sem.at[i]).wait()
                mask_rows(i, i)
                remote(gbuf.at[i], gbuf.at[i], g_send.at[i], g_recv.at[i], sib).start()
            for i in range(per):
                remote(gbuf.at[i], gbuf.at[i], g_send.at[i], g_recv.at[i], sib).wait_send()

        pick(first, send_inputs)
        pick(last, send_cot)
        to_sib.wait_send()
        load_values(wait=True)
        block_rows = count * seq // 2
        act = pbuf.at[:, pl.ds(0, features)]

        def act_rows(index, rows=block_rows):
            return act.at[pl.ds(pl.multiple_of(index * rows, 16), rows), :]

        def make_values(mb, _):
            keep(hbuf, obuf, 0, mb).wait_recv()
            h32 = obuf[mb].astype(F32)
            normed = (h32 * inv_rms(h32)).astype(BF16)
            row = pl.multiple_of(chip * count * seq + mb * seq, 16)
            gram = jnp.zeros((seq, seq), F32)
            for c in range(2):
                cols_c = slice(c * features // 2, (c + 1) * features // 2)
                part = dot_nn(normed, vbuf[:, cols_c]).astype(BF16)
                pbuf[pl.ds(row, seq), cols_c] = part
                gram = gram + dot_nt(part, part)
            grams[mb] = gram
            return 0

        lax.fori_loop(0, count, make_values, 0)

        def ring(way, dist, half):
            step = dist - 1
            origin = lax.rem(chip + chips - step, chips) if way == 0 else lax.rem(chip + step, chips)
            block = act_rows(2 * origin + half)
            dev = up if way == 0 else down
            return remote(block, block, ring_send.at[way, step, half], ring_recv.at[way, step, half], dev)

        def arrived(way, dist, half):
            origin = lax.rem(chip + chips - dist, chips) if way == 0 else lax.rem(chip + dist, chips)
            block = act_rows(2 * origin + half)
            remote(
                block, block, ring_send.at[way, dist - 1, half], ring_recv.at[way, dist - 1, half], up
            ).wait_recv()

        for way in range(2):
            ring(way, 1, 1).start()
        for way in range(2):
            ring(way, 1, 1).wait_send()
            ring(way, 1, 0).start()

        def ring_event(e, _):
            dist, half = lax.div(e + 1, 2), lax.rem(e, 2)
            arrived(0, dist, half)
            pick(jnp.logical_or(dist + 1 < half_ring, half == 0), ring(0, dist + 1, half).start)
            arrived(1, dist, half)
            pick(jnp.logical_or(dist + 1 < half_ring, half == 1), ring(1, dist + 1, half).start)
            return 0

        lax.fori_loop(1, 2 * half_ring - 1, ring_event, 0)
        arrived(0, half_ring, 0)
        arrived(1, half_ring, 1)

        def col_start(owner):
            start = jnp.minimum(lax.div(owner * own_cols, 128) * 128, width - span)
            return pl.multiple_of(start, 128)

        def col_rows(mb):
            return pl.ds(pl.multiple_of(mb * seq, 16), seq)

        def make_parts(mb, _):
            keep(gbuf, qbuf, 1, mb).wait_recv()

            def to_owner(owner):
                remote(
                    qbuf.at[mb, :, pl.ds(col_start(owner), span)], cols.at[chip, col_rows(mb), :],
                    col_send.at[owner], col_recv.at[chip], (sec, 2 * owner),
                ).start()

            g = qbuf[mb]
            part = jnp.sum(grams[mb] * dot_nt(g, g), keepdims=True)
            parts[sec, pl.ds(mb, 1), :] = jnp.broadcast_to(part, (1, 128))
            others(chips, chip, to_owner)
            cols[chip, col_rows(mb), :] = qbuf[mb, :, pl.ds(col_start(chip), span)]
            return 0

        lax.fori_loop(0, count, make_parts, 0)

        def part_copy(to, slot):
            return remote(parts.at[slot], parts.at[slot], part_send.at[to], part_recv.at[slot], (to, dp))

        def scale_copy(to, slot):
            return remote(
                scales.at[slot], scales.at[slot], scale_send.at[to], scale_recv.at[slot], (sec, 2 * to)
            )

        others(secs, sec, lambda to: part_copy(to, sec).start())
        block = count * seq

        def col_copy(owner, source):
            return remote(cols.at[source], cols.at[source], col_send.at[owner], col_recv.at[source], sib)

        def turn(i, _):
            source = lax.rem(chip + i, chips)
            pick(i > 0, col_copy(source, source).wait_recv)
            turned[:, pl.ds(pl.multiple_of(source * block, 128), block)] = cols[source].T
            return 0

        lax.fori_loop(0, chips, turn, 0)
        others(secs, sec, lambda i: part_copy(i, i).wait_recv())
        totals = jnp.sum(parts[...], axis=0)
        scales[chip] = clip_scale / (jnp.sqrt(totals) + GAMMA)
        others(chips, chip, lambda to: scale_copy(to, chip).start())
        others(chips, chip, lambda i: scale_copy(i, i).wait_recv())
        lane = lax.broadcasted_iota(jnp.int32, (1, 128), 1)
        group = 128 // seq
        for tile in range(chips * block // 128):
            row = jnp.zeros((1, 128), F32)
            for k in range(group):
                example = tile * group + k
                value = scales[example // count, example % count:example % count + 1, :]
                row = jnp.where(lax.div(lane, seq) == k, value, row)
            at = slice(tile * 128, (tile + 1) * 128)
            turned[:, at] = (turned[:, at].astype(F32) * row).astype(BF16)

        rows_own = pl.ds(pl.multiple_of(chip * own_cols - col_start(chip), 16), own_cols)
        nout = 4
        cf = features // nout

        def out_copies(c):
            piece = pl.ds(c * cf, cf)
            near = pltpu.make_async_copy(staged.at[pl.ds(0, rows_sl), piece], out_ref.at[:, piece], out_sem.at[c])
            far = remote(
                staged.at[pl.ds(rows_sl, rows_sl), piece], out_ref.at[:, piece],
                out_sem.at[nout + c], out_sem.at[2 * nout], sib,
            )
            return near, far

        for c in range(nout):
            at = slice(c * cf, (c + 1) * cf)
            staged[:, at] = dot_nn(turned[rows_own, :], pbuf[:chips * block, at]).astype(BF16)
            for copy in out_copies(c):
                copy.start()
        for c in range(nout):
            near, far = out_copies(c)
            near.wait()
            far.wait_send()
        others(secs, sec, lambda to: part_copy(to, sec).wait_send())
        others(chips, chip, lambda to: scale_copy(to, chip).wait_send())
        others(chips, chip, lambda to: col_copy(to, chip).wait_send())
        for way in range(2):
            for dist in range(1, half_ring + 1):
                for half in range(2):
                    if (dist < half_ring or half == way) and (dist, half) != (1, 1):
                        ring(way, dist, half).wait_send()

    def relay_core():
        load_w = pltpu.make_async_copy(slice_ref, slice_rows(2 * chip + 1), load_sem.at[0])
        load_in = pltpu.make_async_copy(inp_ref, hbuf.at[pl.ds(per, per)], load_sem.at[1])
        load_cot = pltpu.make_async_copy(cot_ref, gbuf.at[pl.ds(per, per)], load_sem.at[2])
        load_w.start()
        pick(first, load_in.start)
        pick(last, load_cot.start)
        turns = 2 * pieces

        def piece_rows(origin, order):
            index = origin * turns + lax.rem(order + pieces, turns)
            return wbuf.at[pl.ds(pl.multiple_of(index * rows_pc, 16), rows_pc), :]

        def ring(way, dist, order, src=None):
            step = dist - 1
            origin = lax.rem(chip + chips - step, chips) if way == 0 else lax.rem(chip + step, chips)
            block = piece_rows(origin, order)
            dev = up if way == 0 else down
            return remote(
                block if src is None else src, block,
                ring_send.at[way, step, order], ring_recv.at[way, step, order], dev,
            )

        def arrived(way, dist, order):
            origin = lax.rem(chip + chips - dist, chips) if way == 0 else lax.rem(chip + dist, chips)
            block = piece_rows(origin, order)
            remote(
                block, block, ring_send.at[way, dist - 1, order], ring_recv.at[way, dist - 1, order], up
            ).wait_recv()

        for order in range(turns):
            if order == pieces:
                remote(slice_ref, slice_rows(2 * chip), sib_sem.at[0], sib_sem.at[1], sib).wait_recv()
            src = slice_ref.at[pl.ds(order * rows_pc, rows_pc), :] if order < pieces else None
            for way in range(2):
                if order >= pieces:
                    ring(way, 1, order - pieces).wait_send()
                ring(way, 1, order, src).start()
        pick(first, load_in.wait)

        def ready_cot():
            load_cot.wait()
            for i in range(per):
                mask_rows(per + i, i)

        pick(last, ready_cot)
        load_w.wait()
        load_values(wait=True)

        def first_values():
            for i in range(per):
                remote(hbuf.at[i], hbuf.at[i], h_send.at[i], h_recv.at[i], sib).wait_recv()
            h = hbuf[...].reshape(count * seq, width)
            for c in range(2):
                at = slice(c * features // 2, (c + 1) * features // 2)
                tbuf[:count * seq, at] = dot_nn(h, vbuf[:, at]).astype(BF16)

        pick(first, first_values)
        chunks = width // cw

        def chip_gap(index):
            gap = lax.rem(index + chips - chip, chips)
            return jnp.minimum(gap, chips - gap)

        def chunk_level(j):
            rows = 2 * rows_sl
            level = chip_gap(lax.div(cw * j, rows))
            for extra in range(1, (cw - 2) // rows + 2):
                level = jnp.maximum(level, chip_gap(lax.div(jnp.minimum(cw * j + extra * rows, cw * j + cw - 1), rows)))
            return level

        def make_p(level, start, number):
            def chunk(j, _):
                off = pl.multiple_of(j * cw, cw)
                due = jnp.logical_and(j < chunks, chunk_level(jnp.minimum(j, chunks - 1)) == level)

                def run():
                    for m in range(nch):
                        block = dot_nt(vbuf[m * cn:(m + 1) * cn, :], wbuf[pl.ds(off, cw), :])
                        pbuf[m * cn:(m + 1) * cn, pl.ds(off, cw)] = block.astype(BF16)

                def run_first():
                    block = dot_nt(tbuf[:count * seq, :features], wbuf[pl.ds(off, cw), :])
                    ubuf[:, :, pl.ds(off, cw)] = block.reshape(count, seq, cw)

                pick(jnp.logical_and(due, sec > 0), run)
                pick(jnp.logical_and(due, first), run_first)
                return 0

            lax.fori_loop(start, start + number, chunk, 0)

        def ring_event(e, _):
            dist, order = lax.div(e, turns) + 1, lax.rem(e, turns)
            arrived(0, dist, order)
            pick(jnp.logical_or(dist + 1 < half_ring, order < pieces), ring(0, dist + 1, order).start)
            arrived(1, dist, order)
            pick(jnp.logical_or(dist + 1 < half_ring, order >= pieces), ring(1, dist + 1, order).start)
            each = -(-chunks // turns)
            make_p(dist - 1, order * each, each)
            return 0

        lax.fori_loop(0, (half_ring - 1) * turns, ring_event, 0)

        def final_event(k, _):
            arrived(0, half_ring, k)
            arrived(1, half_ring, k + pieces)
            each = -(-chunks // pieces)
            make_p(half_ring - 1, k * each, each)
            return 0

        lax.fori_loop(0, pieces, final_event, 0)
        make_p(half_ring, 0, chunks)

        def make_t():
            def chunk(j, _):
                off = pl.multiple_of(j * cw, cw)
                for m in range(nch):
                    block = dot_nt(wbuf[pl.ds(off, cw), :], vbuf[m * cn:(m + 1) * cn, :])
                    tbuf[pl.ds(off, cw), m * cn:(m + 1) * cn] = block.astype(BF16)
                return 0

            lax.fori_loop(0, width // cw, chunk, 0)

        pick(sec >= tsec, make_t)

        def whole(buf, mb, send, recv, dev):
            return remote(buf.at[mb], buf.at[mb], send.at[mb], recv.at[mb], dev)

        def send_hidden(mb, lo, hi):
            piece = pl.ds(lo, hi - lo)
            remote(
                obuf.at[mb, :, piece], hbuf.at[mb, :, piece], h_send.at[mb], h_recv.at[mb], nxt
            ).start()

        def forward(mb, _):
            whole(hbuf, mb, h_send, h_recv, sib).wait_recv()
            h = hbuf[mb]
            h32 = h.astype(F32)
            r = inv_rms(h32)
            for lo, hi in zip(cuts, cuts[1:]):
                u = dot_tall(h, pbuf[:width, lo:hi])
                ubuf[mb, :, lo:hi] = u
                obuf[mb, :, lo:hi] = (h32[:, lo:hi] + r * u).astype(BF16)
                send_hidden(mb, lo, hi)
            keep(hbuf, obuf, 0, mb).start()
            return 0

        def forward_first(mb, _):
            h32 = hbuf[mb].astype(F32)
            obuf[mb] = (h32 + inv_rms(h32) * ubuf[mb]).astype(BF16)
            for lo, hi in zip(cuts, cuts[1:]):
                send_hidden(mb, lo, hi)
            keep(hbuf, obuf, 0, mb).start()
            return 0

        pick(first, lambda: lax.fori_loop(0, count, forward_first, 0))
        pick(
            jnp.logical_and(sec > 0, sec < secs - 1),
            lambda: lax.fori_loop(0, count, forward, 0),
        )
        pick(jnp.logical_and(sec > 0, sec < tsec), make_t)

        def send_grad(mb, lo, hi):
            piece = pl.ds(lo, hi - lo)

            def to_relay():
                remote(
                    qbuf.at[mb, :, piece], gbuf.at[mb, :, piece], g_send.at[mb], g_recv.at[mb], prv
                ).start()

            def to_helper():
                remote(
                    qbuf.at[mb, :, piece], qbuf.at[mb, :, piece], g_send.at[mb], keep_recv.at[1, mb],
                    (prv[0], prv[1] - 1),
                ).start()

            pick(sec != 1, to_relay)
            pick(sec == 1, to_helper)

        def backward(batch, step, _):
            at = pl.ds(step * batch, batch)
            for i in range(batch):
                whole(gbuf, step * batch + i, g_send, g_recv, sib).wait_recv()
            rows = batch * seq
            g = gbuf[at].reshape(rows, width)
            g32, h32 = g.astype(F32), hbuf[at].reshape(rows, width).astype(F32)
            r = inv_rms(h32)
            coef = jnp.sum(g32 * ubuf[at].reshape(rows, width), axis=-1, keepdims=True) * (r * r * r) * (1.0 / width)
            for lo, hi in zip(cuts, cuts[1:]):
                p = dot_tall(g, tbuf[:, lo:hi])
                result = (g32[:, lo:hi] + r * p - coef * h32[:, lo:hi]).astype(BF16)
                qbuf[at, :, lo:hi] = result.reshape(batch, seq, hi - lo)
                for i in range(batch):
                    send_grad(step * batch + i, lo, hi)
            for i in range(batch):
                keep(gbuf, qbuf, 1, step * batch + i).start()
            return 0

        def backward_last(mb, _):
            pick(mb < per, whole(gbuf, mb, g_send, g_recv, sib).wait_recv)
            keep(gbuf, qbuf, 1, mb).start()
            whole(hbuf, mb, h_send, h_recv, sib).wait_recv()
            keep(hbuf, obuf, 0, mb).start()
            g = gbuf[mb]
            g32, h32 = g.astype(F32), hbuf[mb].astype(F32)
            r = inv_rms(h32)
            dots = jnp.zeros_like(r)
            for lo, hi in zip(cuts, cuts[1:]):
                p = dot_tall(g, tbuf[:, lo:hi])
                ubuf[mb, :, lo:hi] = p
                dots = dots + jnp.sum(p * h32[:, lo:hi], axis=-1, keepdims=True)
            coef = dots * (r * r * r) * (1.0 / width)
            for lo, hi in zip(cuts, cuts[1:]):
                p = ubuf[mb, :, lo:hi]
                qbuf[mb, :, lo:hi] = (g32[:, lo:hi] + r * p - coef * h32[:, lo:hi]).astype(BF16)
                send_grad(mb, lo, hi)
            return 0

        pick(last, lambda: lax.fori_loop(0, count, backward_last, 0))
        pick(
            jnp.logical_and(sec > 0, sec < secs - 2),
            lambda: lax.fori_loop(0, count, functools.partial(backward, 1), 0),
        )
        pick(
            jnp.logical_and(sec > 0, sec == secs - 2),
            lambda: lax.fori_loop(0, count // 2, functools.partial(backward, 2), 0),
        )

        def drain(mb, _):
            pick(sec < secs - 1, whole(hbuf, mb, h_send, h_recv, nxt).wait_send)
            pick(sec > 0, whole(gbuf, mb, g_send, g_recv, prv).wait_send)
            keep(hbuf, obuf, 0, mb).wait_send()
            pick(sec > 0, keep(gbuf, qbuf, 1, mb).wait_send)
            return 0

        lax.fori_loop(0, count, drain, 0)
        for way in range(2):
            for dist in range(1, half_ring + 1):
                for order in range(turns):
                    if dist == half_ring and (order < pieces) != (way == 0):
                        continue
                    if dist > 1 or order >= pieces:
                        ring(way, dist, order).wait_send()
        remote(out_ref, out_ref, out_sem.at[0], out_sem.at[out_sem.shape[0] - 1], sib).wait_recv()

    pick(core == 0, helper_core)
    pick(core == 1, relay_core)


def per_device(inputs, value_weight, output_weight, cotangent, lengths, cw=256, nch=3, tsec=10, cuts=CUTS):
    per, seq, width = inputs.shape
    features = value_weight.shape[2]
    rows_sl = output_weight.shape[1]
    secs, chips = lax.axis_size("section"), lax.axis_size("dp") // 2
    count = 2 * per
    own = width // chips
    span = max(-(-(i * own + own) // 128) - (i * own) // 128 for i in range(chips)) * 128
    clip_scale = math.sqrt(features * width * 1.0 / (count * chips))
    any_spec = pl.BlockSpec(memory_space=pl.ANY)
    dma = pltpu.SemaphoreType.DMA
    tall, wide = max(width, chips * count * seq), max(width, features)
    result = pl.pallas_call(
        functools.partial(relay_kernel, (secs, chips, per, width, cw, nch, tsec, cuts, clip_scale)),
        out_shape=jax.ShapeDtypeStruct((rows_sl, features), BF16),
        in_specs=[any_spec] * 4 + [pl.BlockSpec(memory_space=pltpu.SMEM)],
        out_specs=any_spec,
        scratch_shapes=[
            pltpu.VMEM((width, features), BF16),
            pltpu.VMEM((width, features), BF16),
            pltpu.VMEM((tall, wide), BF16),
            pltpu.VMEM((width, width), BF16),
            pltpu.VMEM((count, seq, width), BF16),
            pltpu.VMEM((count, seq, width), BF16),
            pltpu.VMEM((count, seq, width), BF16),
            pltpu.VMEM((count, seq, width), BF16),
            pltpu.VMEM((count, seq, width), F32),
            pltpu.VMEM((count, seq, seq), F32),
            pltpu.VMEM((chips, count * seq, span), BF16),
            pltpu.VMEM((span, chips * count * seq), BF16),
            pltpu.VMEM((own, features), BF16),
            pltpu.VMEM((secs, count, 128), F32),
            pltpu.VMEM((chips, count, 128), F32),
            dma((per + 7,)),
            dma((2,)),
            dma((2, chips // 2, 6)),
            dma((2, chips // 2, 6)),
            dma((count,)),
            dma((count,)),
            dma((count,)),
            dma((count,)),
            dma((2, count)),
            dma((2, count)),
            dma((chips,)),
            dma((chips,)),
            dma((secs,)),
            dma((secs,)),
            dma((chips,)),
            dma((chips,)),
            dma((9,)),
        ],
        compiler_params=pltpu.CompilerParams(
            collective_id=0, has_side_effects=True, vmem_limit_bytes=60 << 20
        ),
    )(inputs, value_weight[0], output_weight[0], cotangent, lengths)
    return result[None]


def solution(mesh):
    in_specs = (
        P("dp", None, None), P("section", None, None), P("section", "dp", None), P("dp", None, None), P("dp"),
    )
    return jax.shard_map(
        per_device, mesh=mesh, in_specs=in_specs, out_specs=P("section", "dp", None), check_vma=False
    )
```

```python
import functools
import math

import jax
import jax.numpy as jnp
from jax import lax
from jax.experimental import pallas as pl
from jax.experimental.pallas import tpu as pltpu
from jax.sharding import PartitionSpec as P

EPS = 1e-06
GAMMA = 0.01
MESH = pl.DeviceIdType.MESH
CUTS = (0, 1280, 2304)
F32 = jnp.float32
BF16 = jnp.bfloat16


def dot_nn(a, b):
    return lax.dot_general(a, b, (((1,), (0,)), ((), ())), preferred_element_type=F32)


def dot_nt(a, b):
    return lax.dot_general(a, b, (((1,), (1,)), ((), ())), preferred_element_type=F32)


def dot_tall(a, b):
    rows = a.shape[0]
    tall = jnp.concatenate([a] * (128 // rows), axis=0)
    return dot_nn(tall, b)[:rows]


def pick(cond, fn):
    def run():
        fn()

    pl.when(cond)(run)


def relay_kernel(
    cfg, inp_ref, value_ref, slice_ref, cot_ref, len_ref, out_ref,
    vbuf, wbuf, pbuf, tbuf, hbuf, obuf, gbuf, qbuf, ubuf,
    grams, cols, turned, staged, parts, scales,
    load_sem, sib_sem, ring_send, ring_recv, h_send, h_recv, g_send, g_recv,
    keep_send, keep_recv, col_send, col_recv, part_send, part_recv, scale_send, scale_recv, out_sem,
):
    secs, chips, per, width, cw, nch, tsec, cuts, clip_scale = cfg
    seq, features = hbuf.shape[1], vbuf.shape[1]
    span, own_cols = cols.shape[2], width // chips
    half_ring = chips // 2
    rows_sl = slice_ref.shape[0]
    pieces = 3
    rows_pc = rows_sl // pieces
    count = 2 * per
    cn = width // nch
    sec = lax.axis_index("section")
    dp = lax.axis_index("dp")
    chip = lax.div(dp, 2)
    core = lax.rem(dp, 2)
    sib = (sec, dp + 1 - 2 * core)
    up = (sec, lax.rem(chip + 1, chips) * 2 + core)
    down = (sec, lax.rem(chip + chips - 1, chips) * 2 + core)
    nxt = (lax.rem(sec + 1, secs), dp)
    prv = (lax.rem(sec + secs - 1, secs), dp)
    first, last = sec == 0, sec == secs - 1

    part_rows = width // 4

    def load_values(wait):
        for i in range(4):
            rows = pl.ds(i * part_rows, part_rows)
            copy = pltpu.make_async_copy(value_ref.at[rows, :], vbuf.at[rows, :], load_sem.at[per + i])
            copy.wait() if wait else copy.start()

    load_values(wait=False)
    barrier = pltpu.get_barrier_semaphore()

    def greet(dev):
        pl.semaphore_signal(barrier, inc=1, device_id=dev, device_id_type=MESH)

    def others(total, me, fn):
        if total == 16:
            far = (0, 1, 2, 1)
            steps = sorted(range(1, 16), key=lambda i: -far[i // 4] - far[i % 4])
            for i in steps:
                row, col = lax.rem(lax.div(me, 4) + i // 4, 4), lax.rem(lax.rem(me, 4) + i % 4, 4)
                fn(row * 4 + col)
        else:
            for i in sorted(range(1, total), key=lambda i: -min(i, total - i)):
                fn(lax.rem(me + i, total))

    def greet_relay():
        for dev in (up, down, nxt, prv, sib):
            greet(dev)
        pl.semaphore_wait(barrier, 4)

    pick(core == 1, greet_relay)
    pick(core == 0, lambda: pl.semaphore_wait(barrier, 1))

    def remote(src, dst, send, recv, dev):
        return pltpu.make_async_remote_copy(
            src_ref=src, dst_ref=dst, send_sem=send, recv_sem=recv, device_id=dev, device_id_type=MESH
        )

    def slice_rows(index):
        return wbuf.at[pl.ds(pl.multiple_of(index * rows_sl, 16), rows_sl), :]

    def mask_rows(slot, position):
        live = lax.broadcasted_iota(jnp.int32, (seq, 1), 0) < len_ref[position]
        gbuf[slot] = jnp.where(live, gbuf[slot].astype(F32), 0.0).astype(BF16)

    def keep(src, dst, kind, mb):
        return remote(src.at[mb], dst.at[mb], keep_send.at[kind, mb], keep_recv.at[kind, mb], sib)

    def inv_rms(h32):
        return lax.rsqrt(jnp.mean(h32 * h32, axis=-1, keepdims=True) + EPS)

    def helper_core():
        to_sib = remote(slice_ref, slice_rows(2 * chip), sib_sem.at[0], sib_sem.at[1], sib)
        to_sib.start()
        def send_inputs():
            for i in range(per):
                remote(inp_ref.at[i], hbuf.at[i], h_send.at[i], h_recv.at[i], sib).start()
            for i in range(per):
                remote(inp_ref.at[i], hbuf.at[i], h_send.at[i], h_recv.at[i], sib).wait_send()

        def send_cot():
            for i in range(per):
                pltpu.make_async_copy(cot_ref.at[i], gbuf.at[i], load_sem.at[i]).start()
            for i in range(per):
                pltpu.make_async_copy(cot_ref.at[i], gbuf.at[i], load_sem.at[i]).wait()
                mask_rows(i, i)
                remote(gbuf.at[i], gbuf.at[i], g_send.at[i], g_recv.at[i], sib).start()
            for i in range(per):
                remote(gbuf.at[i], gbuf.at[i], g_send.at[i], g_recv.at[i], sib).wait_send()

        pick(first, send_inputs)
        pick(last, send_cot)
        to_sib.wait_send()
        load_values(wait=True)
        block_rows = count * seq // 2
        act = pbuf.at[:, pl.ds(0, features)]

        def act_rows(index, rows=block_rows):
            return act.at[pl.ds(pl.multiple_of(index * rows, 16), rows), :]

        def make_values(mb, _):
            keep(hbuf, obuf, 0, mb).wait_recv()
            h32 = obuf[mb].astype(F32)
            normed = (h32 * inv_rms(h32)).astype(BF16)
            row = pl.multiple_of(chip * count * seq + mb * seq, 16)
            gram = jnp.zeros((seq, seq), F32)
            for c in range(2):
                cols_c = slice(c * features // 2, (c + 1) * features // 2)
                part = dot_nn(normed, vbuf[:, cols_c]).astype(BF16)
                pbuf[pl.ds(row, seq), cols_c] = part
                gram = gram + dot_nt(part, part)
            grams[mb] = gram
            return 0

        lax.fori_loop(0, count, make_values, 0)

        def ring(way, dist, half):
            step = dist - 1
            origin = lax.rem(chip + chips - step, chips) if way == 0 else lax.rem(chip + step, chips)
            block = act_rows(2 * origin + half)
            dev = up if way == 0 else down
            return remote(block, block, ring_send.at[way, step, half], ring_recv.at[way, step, half], dev)

        def arrived(way, dist, half):
            origin = lax.rem(chip + chips - dist, chips) if way == 0 else lax.rem(chip + dist, chips)
            block = act_rows(2 * origin + half)
            remote(
                block, block, ring_send.at[way, dist - 1, half], ring_recv.at[way, dist - 1, half], up
            ).wait_recv()

        for way in range(2):
            ring(way, 1, 1).start()
        for way in range(2):
            ring(way, 1, 1).wait_send()
            ring(way, 1, 0).start()

        def ring_event(e, _):
            dist, half = lax.div(e + 1, 2), lax.rem(e, 2)
            arrived(0, dist, half)
            pick(jnp.logical_or(dist + 1 < half_ring, half == 0), ring(0, dist + 1, half).start)
            arrived(1, dist, half)
            pick(jnp.logical_or(dist + 1 < half_ring, half == 1), ring(1, dist + 1, half).start)
            return 0

        lax.fori_loop(1, 2 * half_ring - 1, ring_event, 0)
        arrived(0, half_ring, 0)
        arrived(1, half_ring, 1)

        def col_start(owner):
            start = jnp.minimum(lax.div(owner * own_cols, 128) * 128, width - span)
            return pl.multiple_of(start, 128)

        def col_rows(mb):
            return pl.ds(pl.multiple_of(mb * seq, 16), seq)

        def send_cols(mb):
            def to_owner(owner):
                remote(
                    qbuf.at[mb, :, pl.ds(col_start(owner), span)], cols.at[chip, col_rows(mb), :],
                    col_send.at[owner], col_recv.at[chip], (sec, 2 * owner),
                ).start()

            others(chips, chip, to_owner)
            cols[chip, col_rows(mb), :] = qbuf[mb, :, pl.ds(col_start(chip), span)]

        def make_parts(mb, _):
            keep(gbuf, qbuf, 1, mb).wait_recv()
            g = qbuf[mb]
            part = jnp.sum(grams[mb] * dot_nt(g, g), keepdims=True)
            parts[sec, pl.ds(mb, 1), :] = jnp.broadcast_to(part, (1, 128))
            pick(mb < count - 1, lambda: send_cols(mb))
            return 0

        lax.fori_loop(0, count, make_parts, 0)

        def part_copy(to, slot):
            return remote(parts.at[slot], parts.at[slot], part_send.at[to], part_recv.at[slot], (to, dp))

        def scale_copy(to, slot):
            return remote(
                scales.at[slot], scales.at[slot], scale_send.at[to], scale_recv.at[slot], (sec, 2 * to)
            )

        others(secs, sec, lambda to: part_copy(to, sec).start())
        send_cols(count - 1)
        others(secs, sec, lambda i: part_copy(i, i).wait_recv())
        totals = jnp.sum(parts[...], axis=0)
        scales[chip] = clip_scale / (jnp.sqrt(totals) + GAMMA)
        others(chips, chip, lambda to: scale_copy(to, chip).start())
        block = count * seq

        def col_copy(owner, source):
            return remote(cols.at[source], cols.at[source], col_send.at[owner], col_recv.at[source], sib)

        def turn(i, _):
            source = lax.rem(chip + i, chips)
            pick(i > 0, col_copy(source, source).wait_recv)
            turned[:, pl.ds(pl.multiple_of(source * block, 128), block)] = cols[source].T
            return 0

        lax.fori_loop(0, chips, turn, 0)
        others(chips, chip, lambda i: scale_copy(i, i).wait_recv())
        lane = lax.broadcasted_iota(jnp.int32, (1, 128), 1)
        group = 128 // seq
        for tile in range(chips * block // 128):
            row = jnp.zeros((1, 128), F32)
            for k in range(group):
                example = tile * group + k
                value = scales[example // count, example % count:example % count + 1, :]
                row = jnp.where(lax.div(lane, seq) == k, value, row)
            at = slice(tile * 128, (tile + 1) * 128)
            turned[:, at] = (turned[:, at].astype(F32) * row).astype(BF16)

        rows_own = pl.ds(pl.multiple_of(chip * own_cols - col_start(chip), 16), own_cols)
        nout = 4
        cf = features // nout

        def out_copies(c):
            piece = pl.ds(c * cf, cf)
            near = pltpu.make_async_copy(staged.at[pl.ds(0, rows_sl), piece], out_ref.at[:, piece], out_sem.at[c])
            far = remote(
                staged.at[pl.ds(rows_sl, rows_sl), piece], out_ref.at[:, piece],
                out_sem.at[nout + c], out_sem.at[2 * nout], sib,
            )
            return near, far

        for c in range(nout):
            at = slice(c * cf, (c + 1) * cf)
            staged[:, at] = dot_nn(turned[rows_own, :], pbuf[:chips * block, at]).astype(BF16)
            for copy in out_copies(c):
                copy.start()
        for c in range(nout):
            near, far = out_copies(c)
            near.wait()
            far.wait_send()
        others(secs, sec, lambda to: part_copy(to, sec).wait_send())
        others(chips, chip, lambda to: scale_copy(to, chip).wait_send())
        others(chips, chip, lambda to: col_copy(to, chip).wait_send())
        for way in range(2):
            for dist in range(1, half_ring + 1):
                for half in range(2):
                    if (dist < half_ring or half == way) and (dist, half) != (1, 1):
                        ring(way, dist, half).wait_send()

    def relay_core():
        load_w = pltpu.make_async_copy(slice_ref, slice_rows(2 * chip + 1), load_sem.at[0])
        load_in = pltpu.make_async_copy(inp_ref, hbuf.at[pl.ds(per, per)], load_sem.at[1])
        load_cot = pltpu.make_async_copy(cot_ref, gbuf.at[pl.ds(per, per)], load_sem.at[2])
        load_w.start()
        pick(first, load_in.start)
        pick(last, load_cot.start)
        turns = 2 * pieces

        def piece_rows(origin, order):
            index = origin * turns + lax.rem(order + pieces, turns)
            return wbuf.at[pl.ds(pl.multiple_of(index * rows_pc, 16), rows_pc), :]

        def ring(way, dist, order, src=None):
            step = dist - 1
            origin = lax.rem(chip + chips - step, chips) if way == 0 else lax.rem(chip + step, chips)
            block = piece_rows(origin, order)
            dev = up if way == 0 else down
            return remote(
                block if src is None else src, block,
                ring_send.at[way, step, order], ring_recv.at[way, step, order], dev,
            )

        def arrived(way, dist, order):
            origin = lax.rem(chip + chips - dist, chips) if way == 0 else lax.rem(chip + dist, chips)
            block = piece_rows(origin, order)
            remote(
                block, block, ring_send.at[way, dist - 1, order], ring_recv.at[way, dist - 1, order], up
            ).wait_recv()

        for order in range(turns):
            if order == pieces:
                remote(slice_ref, slice_rows(2 * chip), sib_sem.at[0], sib_sem.at[1], sib).wait_recv()
            src = slice_ref.at[pl.ds(order * rows_pc, rows_pc), :] if order < pieces else None
            for way in range(2):
                if order >= pieces:
                    ring(way, 1, order - pieces).wait_send()
                ring(way, 1, order, src).start()
        pick(first, load_in.wait)

        def ready_cot():
            load_cot.wait()
            for i in range(per):
                mask_rows(per + i, i)

        pick(last, ready_cot)
        load_w.wait()
        load_values(wait=True)

        def first_values():
            for i in range(per):
                remote(hbuf.at[i], hbuf.at[i], h_send.at[i], h_recv.at[i], sib).wait_recv()
            h = hbuf[...].reshape(count * seq, width)
            for c in range(2):
                at = slice(c * features // 2, (c + 1) * features // 2)
                tbuf[:count * seq, at] = dot_nn(h, vbuf[:, at]).astype(BF16)

        pick(first, first_values)
        chunks = width // cw

        def chip_gap(index):
            gap = lax.rem(index + chips - chip, chips)
            return jnp.minimum(gap, chips - gap)

        def chunk_level(j):
            rows = 2 * rows_sl
            level = chip_gap(lax.div(cw * j, rows))
            for extra in range(1, (cw - 2) // rows + 2):
                level = jnp.maximum(level, chip_gap(lax.div(jnp.minimum(cw * j + extra * rows, cw * j + cw - 1), rows)))
            return level

        def make_p(level, start, number):
            def chunk(j, _):
                off = pl.multiple_of(j * cw, cw)
                due = jnp.logical_and(j < chunks, chunk_level(jnp.minimum(j, chunks - 1)) == level)

                def run():
                    for m in range(nch):
                        block = dot_nt(vbuf[m * cn:(m + 1) * cn, :], wbuf[pl.ds(off, cw), :])
                        pbuf[m * cn:(m + 1) * cn, pl.ds(off, cw)] = block.astype(BF16)

                def run_first():
                    block = dot_nt(tbuf[:count * seq, :features], wbuf[pl.ds(off, cw), :])
                    ubuf[:, :, pl.ds(off, cw)] = block.reshape(count, seq, cw)

                pick(jnp.logical_and(due, sec > 0), run)
                pick(jnp.logical_and(due, first), run_first)
                return 0

            lax.fori_loop(start, start + number, chunk, 0)

        def ring_event(e, _):
            dist, order = lax.div(e, turns) + 1, lax.rem(e, turns)
            arrived(0, dist, order)
            pick(jnp.logical_or(dist + 1 < half_ring, order < pieces), ring(0, dist + 1, order).start)
            arrived(1, dist, order)
            pick(jnp.logical_or(dist + 1 < half_ring, order >= pieces), ring(1, dist + 1, order).start)
            each = -(-chunks // turns)
            make_p(dist - 1, order * each, each)
            return 0

        lax.fori_loop(0, (half_ring - 1) * turns, ring_event, 0)

        def final_event(k, _):
            arrived(0, half_ring, k)
            arrived(1, half_ring, k + pieces)
            each = -(-chunks // pieces)
            make_p(half_ring - 1, k * each, each)
            return 0

        lax.fori_loop(0, pieces, final_event, 0)
        make_p(half_ring, 0, chunks)

        def make_t():
            def chunk(j, _):
                off = pl.multiple_of(j * cw, cw)
                for m in range(nch):
                    block = dot_nt(wbuf[pl.ds(off, cw), :], vbuf[m * cn:(m + 1) * cn, :])
                    tbuf[pl.ds(off, cw), m * cn:(m + 1) * cn] = block.astype(BF16)
                return 0

            lax.fori_loop(0, width // cw, chunk, 0)

        pick(sec >= tsec, make_t)

        def whole(buf, mb, send, recv, dev):
            return remote(buf.at[mb], buf.at[mb], send.at[mb], recv.at[mb], dev)

        def send_hidden(mb, lo, hi):
            piece = pl.ds(lo, hi - lo)
            remote(
                obuf.at[mb, :, piece], hbuf.at[mb, :, piece], h_send.at[mb], h_recv.at[mb], nxt
            ).start()

        def forward(mb, _):
            whole(hbuf, mb, h_send, h_recv, sib).wait_recv()
            h = hbuf[mb]
            h32 = h.astype(F32)
            r = inv_rms(h32)
            for lo, hi in zip(cuts, cuts[1:]):
                u = dot_tall(h, pbuf[:width, lo:hi])
                ubuf[mb, :, lo:hi] = u
                obuf[mb, :, lo:hi] = (h32[:, lo:hi] + r * u).astype(BF16)
                send_hidden(mb, lo, hi)
            keep(hbuf, obuf, 0, mb).start()
            return 0

        def forward_first(mb, _):
            h32 = hbuf[mb].astype(F32)
            obuf[mb] = (h32 + inv_rms(h32) * ubuf[mb]).astype(BF16)
            for lo, hi in zip(cuts, cuts[1:]):
                send_hidden(mb, lo, hi)
            keep(hbuf, obuf, 0, mb).start()
            return 0

        pick(first, lambda: lax.fori_loop(0, count, forward_first, 0))
        pick(
            jnp.logical_and(sec > 0, sec < secs - 1),
            lambda: lax.fori_loop(0, count, forward, 0),
        )
        pick(jnp.logical_and(sec > 0, sec < tsec), make_t)

        def send_grad(mb, lo, hi):
            piece = pl.ds(lo, hi - lo)

            def to_relay():
                remote(
                    qbuf.at[mb, :, piece], gbuf.at[mb, :, piece], g_send.at[mb], g_recv.at[mb], prv
                ).start()

            def to_helper():
                remote(
                    qbuf.at[mb, :, piece], qbuf.at[mb, :, piece], g_send.at[mb], keep_recv.at[1, mb],
                    (prv[0], prv[1] - 1),
                ).start()

            pick(sec != 1, to_relay)
            pick(sec == 1, to_helper)

        def backward(batch, step, _):
            at = pl.ds(step * batch, batch)
            for i in range(batch):
                whole(gbuf, step * batch + i, g_send, g_recv, sib).wait_recv()
            rows = batch * seq
            g = gbuf[at].reshape(rows, width)
            g32, h32 = g.astype(F32), hbuf[at].reshape(rows, width).astype(F32)
            r = inv_rms(h32)
            coef = jnp.sum(g32 * ubuf[at].reshape(rows, width), axis=-1, keepdims=True) * (r * r * r) * (1.0 / width)
            for lo, hi in zip(cuts, cuts[1:]):
                p = dot_tall(g, tbuf[:, lo:hi])
                result = (g32[:, lo:hi] + r * p - coef * h32[:, lo:hi]).astype(BF16)
                qbuf[at, :, lo:hi] = result.reshape(batch, seq, hi - lo)
                for i in range(batch):
                    send_grad(step * batch + i, lo, hi)
            for i in range(batch):
                keep(gbuf, qbuf, 1, step * batch + i).start()
            return 0

        def backward_last(mb, _):
            pick(mb < per, whole(gbuf, mb, g_send, g_recv, sib).wait_recv)
            keep(gbuf, qbuf, 1, mb).start()
            whole(hbuf, mb, h_send, h_recv, sib).wait_recv()
            keep(hbuf, obuf, 0, mb).start()
            g = gbuf[mb]
            g32, h32 = g.astype(F32), hbuf[mb].astype(F32)
            r = inv_rms(h32)
            dots = jnp.zeros_like(r)
            for lo, hi in zip(cuts, cuts[1:]):
                p = dot_tall(g, tbuf[:, lo:hi])
                ubuf[mb, :, lo:hi] = p
                dots = dots + jnp.sum(p * h32[:, lo:hi], axis=-1, keepdims=True)
            coef = dots * (r * r * r) * (1.0 / width)
            for lo, hi in zip(cuts, cuts[1:]):
                p = ubuf[mb, :, lo:hi]
                qbuf[mb, :, lo:hi] = (g32[:, lo:hi] + r * p - coef * h32[:, lo:hi]).astype(BF16)
                send_grad(mb, lo, hi)
            return 0

        pick(last, lambda: lax.fori_loop(0, count, backward_last, 0))
        pick(
            jnp.logical_and(sec > 0, sec < secs - 2),
            lambda: lax.fori_loop(0, count, functools.partial(backward, 1), 0),
        )
        pick(
            jnp.logical_and(sec > 0, sec == secs - 2),
            lambda: lax.fori_loop(0, count // 2, functools.partial(backward, 2), 0),
        )

        def drain(mb, _):
            pick(sec < secs - 1, whole(hbuf, mb, h_send, h_recv, nxt).wait_send)
            pick(sec > 0, whole(gbuf, mb, g_send, g_recv, prv).wait_send)
            keep(hbuf, obuf, 0, mb).wait_send()
            pick(sec > 0, keep(gbuf, qbuf, 1, mb).wait_send)
            return 0

        lax.fori_loop(0, count, drain, 0)
        for way in range(2):
            for dist in range(1, half_ring + 1):
                for order in range(turns):
                    if dist == half_ring and (order < pieces) != (way == 0):
                        continue
                    if dist > 1 or order >= pieces:
                        ring(way, dist, order).wait_send()
        remote(out_ref, out_ref, out_sem.at[0], out_sem.at[out_sem.shape[0] - 1], sib).wait_recv()

    pick(core == 0, helper_core)
    pick(core == 1, relay_core)


def per_device(inputs, value_weight, output_weight, cotangent, lengths, cw=256, nch=3, tsec=10, cuts=CUTS):
    per, seq, width = inputs.shape
    features = value_weight.shape[2]
    rows_sl = output_weight.shape[1]
    secs, chips = lax.axis_size("section"), lax.axis_size("dp") // 2
    count = 2 * per
    own = width // chips
    span = max(-(-(i * own + own) // 128) - (i * own) // 128 for i in range(chips)) * 128
    clip_scale = math.sqrt(features * width * 1.0 / (count * chips))
    any_spec = pl.BlockSpec(memory_space=pl.ANY)
    dma = pltpu.SemaphoreType.DMA
    tall, wide = max(width, chips * count * seq), max(width, features)
    result = pl.pallas_call(
        functools.partial(relay_kernel, (secs, chips, per, width, cw, nch, tsec, cuts, clip_scale)),
        out_shape=jax.ShapeDtypeStruct((rows_sl, features), BF16),
        in_specs=[any_spec] * 4 + [pl.BlockSpec(memory_space=pltpu.SMEM)],
        out_specs=any_spec,
        scratch_shapes=[
            pltpu.VMEM((width, features), BF16),
            pltpu.VMEM((width, features), BF16),
            pltpu.VMEM((tall, wide), BF16),
            pltpu.VMEM((width, width), BF16),
            pltpu.VMEM((count, seq, width), BF16),
            pltpu.VMEM((count, seq, width), BF16),
            pltpu.VMEM((count, seq, width), BF16),
            pltpu.VMEM((count, seq, width), BF16),
            pltpu.VMEM((count, seq, width), F32),
            pltpu.VMEM((count, seq, seq), F32),
            pltpu.VMEM((chips, count * seq, span), BF16),
            pltpu.VMEM((span, chips * count * seq), BF16),
            pltpu.VMEM((own, features), BF16),
            pltpu.VMEM((secs, count, 128), F32),
            pltpu.VMEM((chips, count, 128), F32),
            dma((per + 7,)),
            dma((2,)),
            dma((2, chips // 2, 6)),
            dma((2, chips // 2, 6)),
            dma((count,)),
            dma((count,)),
            dma((count,)),
            dma((count,)),
            dma((2, count)),
            dma((2, count)),
            dma((chips,)),
            dma((chips,)),
            dma((secs,)),
            dma((secs,)),
            dma((chips,)),
            dma((chips,)),
            dma((9,)),
        ],
        compiler_params=pltpu.CompilerParams(
            collective_id=0, has_side_effects=True, vmem_limit_bytes=60 << 20
        ),
    )(inputs, value_weight[0], output_weight[0], cotangent, lengths)
    return result[None]


def solution(mesh):
    in_specs = (
        P("dp", None, None), P("section", None, None), P("section", "dp", None), P("dp", None, None), P("dp"),
    )
    return jax.shard_map(
        per_device, mesh=mesh, in_specs=in_specs, out_specs=P("section", "dp", None), check_vma=False
    )
```
